32 devices in a mesh: slab: 8 (over y, x, core), img: 4 (over z).
Axes of the slice: x: 2, y: 2, z: 4, core: 2. Of those that a mesh axis runs over, the one named last changes fastest.
Arguments:
- volume: float32 [32, 1024, 1024], P('img', 'slab'), may hold values from -6 to 6
- blk_plane: int32 [128, 8], replicated, may hold values from 0 to 30, all different within a row; in each aligned block of 4 rows (0 to 3, 4 to 7, ...) at most 2 rows name the same one
- blk_row: int32 [128, 8], replicated, may hold values from 0 to 1022
- blk_col: int32 [128, 8], replicated, may hold values from 0 to 7
- frac_plane: float32 [128, 8], replicated, may hold values from 0 to 1
- frac_row: float32 [128, 8], replicated, may hold values from 0 to 1
- defocus: float32 [128], replicated, may hold values from 0.5 to 4
Outputs:
- slices: float32 [128, 8, 2, 128], P(('slab', 'img'))
The draws below stay inside these ranges and needn't reach their ends.
Inputs may be any that keep to these rules, and one draw needn't show every extreme that they name: `blk_plane`: the blocks of one image name different lower planes. Among the 4 images of one device (aligned groups of images), no plane is the lower plane of more than 2 blocks, and some plane reaches 2.
All inputs are finite; a program needn't handle non-finite values.
Results may differ from the reference program's by a relative error of at most 0.0003.
Values sent between devices are 32-bit elements; how exact they have to be, the bound alone decides.
A program may use at most 128 MiB of HBM per device.

```python
import math
import jax
import jax.numpy as jnp
import numpy as np
from jax import lax

BOX = 1024
LANES = 128
IMG_DEV = 4
IMG_BLK = 8
MOST = 2
PLANES = 32
NIMG = 128


def touch_ends(array, stream_key, least, top_value):
    index_at = [jax.random.randint(jax.random.fold_in(stream_key, axis), (), 0, length) for axis, length in enumerate(array.shape)]
    main_axis = array.shape.index(max(array.shape))
    next_to = index_at[:main_axis] + [(index_at[main_axis] + 1) % array.shape[main_axis]] + index_at[main_axis + 1:]
    return array.at[tuple(index_at)].set(least).at[tuple(next_to)].set(top_value)


def steps_of(own_key, dims, pieces, smallest, largest):
    factor_of, own = 1.0, jax.random.fold_in(own_key, 6)
    for axis_at, blocks in pieces:
        draws = jnp.exp(jax.random.uniform(jax.random.fold_in(own, axis_at), (blocks,), jnp.float32, smallest / len(pieces), largest / len(pieces)))
        factor_of = factor_of * jnp.repeat(draws, dims[axis_at] // blocks).reshape([-1 if axis == axis_at else 1 for axis in range(len(dims))])
    return factor_of


def routed_block(stream_key, own, number, rows, number_of, top, reach, lean):
    sequence = jax.random.permutation(stream_key, number_of)
    crowded, usual = shares(number_of, rows * top, reach, lean, True), shares(number_of, rows * top, reach, lean, False)
    places = jnp.arange(number_of)

    def named(sizes, turn):
        used = int((sizes > 0).sum())
        fixed = max(1, used // 4)
        passed = fixed + (places - fixed + turn * (used - fixed)) % max(1, number_of - fixed)
        return jnp.zeros((number_of,), jnp.int32).at[sequence[jnp.where(places < fixed, places, passed)]].set(jnp.asarray(sizes, jnp.int32))

    sizes = jnp.where(number % 4 == 0, named(crowded, number // 4), named(usual, number - number // 4 - 1))
    mixed = jax.random.permutation(jax.random.fold_in(own, 3), number_of)
    giver, receiver = mixed[0:number_of // 2 * 2:2], mixed[1:number_of // 2 * 2:2]
    margin = jnp.minimum(sizes[giver] - 1, reach - sizes[receiver]) // 2
    margin = jnp.where((giver == sequence[0]) | (receiver == sequence[0]) | (sizes[receiver] == 0), 0, jnp.maximum(margin, 0))
    passed = jax.random.randint(jax.random.fold_in(own, 4), (number_of // 2,), 0, 1 << 20) % (margin + 1)
    sizes = sizes.at[giver].add(-passed).at[receiver].add(passed)
    labels = jnp.searchsorted(jnp.cumsum(sizes), jnp.arange(rows * top), side="right").astype(jnp.int32)
    grid = labels.reshape(top, rows).T
    grid = grid[jax.random.permutation(jax.random.fold_in(own, 1), rows)]
    turn = jax.random.randint(jax.random.fold_in(own, 2), (rows, 1), 0, top)
    return jnp.take_along_axis(grid, (jnp.arange(top)[None, :] + turn) % top, axis=1)


def shares(number_of, total, most, skew, full):
    loads = [(1 << 20) // math.isqrt(grade ** skew) + 1 for grade in range(1, number_of + 1)]
    largest = most if full else min(most, max(-(-total // number_of), total * loads[0] // sum(loads)))
    least = 1 if total - largest >= number_of - 1 else 0
    counts, spare = [largest] + [least] * (number_of - 1), total - largest - least * (number_of - 1)
    while spare > 0:
        free = [i for i in range(1, number_of) if counts[i] < largest] or [i for i in range(1, number_of) if counts[i] < most]
        pool, left = sum([loads[i] for i in free]), spare
        for i in free:
            more = min(most - counts[i], max(1, left * loads[i] // pool), spare)
            counts[i] = counts[i] + more
            spare = spare - more
    return np.array(counts)


def scatter_about(rng, shape, deviation, limit, split=(), held_as=jnp.bfloat16):
    values = deviation * jax.random.normal(rng, shape, jnp.float32)
    if split:
        values = values * steps_of(rng, shape, split, -0.22, 0.18)
    return jnp.clip(values, -limit, limit).astype(held_as)


def setup_inputs(seed: int = 0) -> dict:
    key_of = jax.random.split(jax.random.key(seed), 8)
    volume = scatter_about(key_of[0], (PLANES, BOX, BOX), 1.0, 6.0, ((0, 4), (1, 8)), jnp.float32)
    blk_plane_keys = jax.random.split(jax.random.fold_in(key_of[1], 1), NIMG // IMG_DEV)
    blk_plane_turns = jax.random.permutation(jax.random.fold_in(key_of[1], 3), NIMG // IMG_DEV)
    blk_plane = jax.vmap(lambda own, number: routed_block(jax.random.fold_in(key_of[1], 2), own, number, IMG_DEV, PLANES - 1, IMG_BLK, MOST, 2))(blk_plane_keys, blk_plane_turns).reshape((NIMG, IMG_BLK))
    blk_row = touch_ends(jax.random.randint(key_of[2], (NIMG, IMG_BLK), 0, BOX - 1), jax.random.fold_in(key_of[2], 1), 0, (BOX - 1) - 1).astype(jnp.int32)
    blk_col = touch_ends(jax.random.randint(key_of[3], (NIMG, IMG_BLK), 0, BOX // LANES), jax.random.fold_in(key_of[3], 1), 0, (BOX // LANES) - 1).astype(jnp.int32)
    frac_plane = jnp.clip(jax.random.uniform(key_of[4], (NIMG, IMG_BLK), jnp.float32, 0.0, 1.0), 0.0, 1.0)
    frac_row = jnp.clip(jax.random.uniform(key_of[5], (NIMG, IMG_BLK), jnp.float32, 0.0, 1.0), 0.0, 1.0)
    defocus = jnp.clip(jnp.exp(jax.random.uniform(key_of[6], (NIMG,), jnp.float32, math.log(0.5), math.log(4.0))), 0.5, 4.0)
    return {"volume": volume, "blk_plane": blk_plane, "blk_row": blk_row, "blk_col": blk_col, "frac_plane": frac_plane, "frac_row": frac_row, "defocus": defocus}


CTF_SCALE = 20.0
CTF_PHASE = 0.07


def reference(volume, blk_plane, blk_row, blk_col, frac_plane, frac_row, defocus):
    plane_idx = blk_plane.reshape(-1).astype(jnp.int32)
    rows = blk_row.reshape(-1).astype(jnp.int32)
    cols = blk_col.reshape(-1).astype(jnp.int32)
    frac_z = frac_plane.reshape(-1)
    frac_y = frac_row.reshape(-1)[:, None]
    focus = jnp.repeat(defocus, IMG_BLK)
    lane = jnp.arange(LANES, dtype=jnp.int32)
    column_x = cols[:, None] * LANES + lane[None, :]
    fold_x = jnp.minimum(column_x, BOX - column_x).astype(jnp.float32)
    fold_y = jnp.minimum(rows, BOX - rows).astype(jnp.float32)
    wave_sq = (fold_x * fold_x + (fold_y * fold_y)[:, None]) / float(BOX * BOX)
    ctf_value = -jnp.sin(CTF_SCALE * focus[:, None] * wave_sq + CTF_PHASE)
    per_row = BOX // LANES
    index_low = rows * per_row + cols
    index_high = index_low + per_row

    def step(carry, item):
        plane, here = item
        spectrum = jnp.fft.fft2(plane, norm="ortho")
        flat_real = jnp.real(spectrum).reshape(-1, LANES)
        flat_imag = jnp.imag(spectrum).reshape(-1, LANES)
        weight = jnp.where(plane_idx == here, 1.0 - frac_z, 0.0) + jnp.where(plane_idx + 1 == here, frac_z, 0.0)
        scale = weight[:, None] * ctf_value
        part_real = scale * ((1.0 - frac_y) * flat_real[index_low] + frac_y * flat_real[index_high])
        part_imag = scale * ((1.0 - frac_y) * flat_imag[index_low] + frac_y * flat_imag[index_high])
        return (carry[0] + part_real, carry[1] + part_imag), None

    empty = jnp.zeros((plane_idx.shape[0], LANES), jnp.float32)
    (total_real, total_imag), _ = lax.scan(step, (empty, empty), (volume, jnp.arange(PLANES, dtype=jnp.int32)))
    stacked = jnp.stack([total_real, total_imag], axis=1)
    return stacked.reshape(NIMG, IMG_BLK, 2, LANES)
```

```python
import functools
import math

import jax
import jax.numpy as jnp
import ml_dtypes
import numpy as np
from jax import lax
from jax.experimental import pallas as pl
from jax.experimental.pallas import tpu as pltpu
from jax.sharding import PartitionSpec as P

LANES = 128
CTF_SCALE = 20.0
CTF_PHASE = 0.07
MOST = 2
MESH = pl.DeviceIdType.MESH
F32 = jnp.float32
BF16 = jnp.bfloat16


def wave_coefficients():
    grid = 0.5 * np.cos(np.linspace(0.0, np.pi, 4001))
    grid = grid[grid > 1e-6]
    basis = (4 * grid * grid)[:, None] ** np.arange(8)
    scale = 4.0 ** np.arange(8)
    cos_c = np.linalg.lstsq(basis, np.cos(2 * np.pi * grid), rcond=None)[0] * scale
    sin_c = np.linalg.lstsq(basis[:, :7] * grid[:, None], np.sin(2 * np.pi * grid), rcond=None)[0] * scale[:7]
    return [float(v) for v in cos_c], [float(v) for v in sin_c]


COS_C, SIN_C = wave_coefficients()


def horner(coefficients, value):
    total = jnp.full_like(value, coefficients[-1])
    for c in coefficients[-2::-1]:
        total = total * value + c
    return total


def wave(turns):
    part = turns - jnp.round(turns)
    square = part * part
    return horner(COS_C, square), part * horner(SIN_C, square)


def split_table(table):
    high = table.astype(ml_dtypes.bfloat16)
    low = (table - high.astype(np.float64)).astype(ml_dtypes.bfloat16)
    return high, low


def column_table(box):
    half = box // 2
    phase = (np.arange(box)[:, None] * np.arange(half)[None, :]) % box
    angle = phase * (2.0 * np.pi / box)
    real, imag = np.cos(angle), -np.sin(angle)
    imag[:, 0] = 1.0 - 2.0 * (np.arange(box) % 2)
    table = np.stack([real.reshape(box, -1, LANES), imag.reshape(box, -1, LANES)], axis=2)
    return split_table(table.reshape(box, box))


def halves(value):
    high = value.astype(BF16)
    low = (value - high.astype(F32)).astype(BF16)
    return high, low


def dot(a, b):
    return jnp.dot(a, b, preferred_element_type=F32)


def kernel(
    dims, meta_ref, vol_hbm, high_hbm, low_hbm, out_ref,
    vol, t_high, t_low, z_high, z_low, g_high, g_low, cols, stage, recv, red, recv2,
    vol_sem, tab_sem, send_sem, recv_sem, send2_sem, recv2_sem,
):
    n_slab, n_img, n_plane, n_row, box, n_group, n_blk, per_step = dims
    n_pair = n_plane + 1
    n_slot = MOST * n_group
    tile = MOST * n_img
    half_blocks = box // LANES // 2
    s, i = lax.axis_index("slab"), lax.axis_index("img")

    tab_copies = [
        pltpu.make_async_copy(high_hbm, t_high, tab_sem.at[0]),
        pltpu.make_async_copy(low_hbm, t_low, tab_sem.at[1]),
    ]

    def vol_copy(q):
        return pltpu.make_async_copy(vol_hbm.at[q], vol.at[q], vol_sem.at[q])

    tab_copies[0].start()
    vol_copy(0).start()
    tab_copies[1].start()
    for q in range(1, n_plane):
        vol_copy(q).start()

    barrier = pltpu.get_barrier_semaphore()
    for d in range(1, n_slab):
        pl.semaphore_signal(barrier, inc=1, device_id=(lax.rem(s + d, n_slab), i), device_id_type=MESH)
    for d in range(1, n_img):
        pl.semaphore_signal(barrier, inc=1, device_id=(s, lax.rem(i + d, n_img)), device_id_type=MESH)

    zero_rows = jnp.zeros((n_row, box), BF16)
    for ref in (z_high, z_low):
        ref[pl.ds(0, n_row)] = zero_rows
        ref[pl.ds((n_plane + 1) * n_row, n_row)] = zero_rows
    red[...] = jnp.zeros_like(red)

    lane = lax.broadcasted_iota(jnp.int32, (1, n_row), 1)
    y = (lane + s * n_row).astype(F32)
    step_cos, step_sin = wave(y * (1.0 / box))
    blk = lax.broadcasted_iota(jnp.int32, (n_slot, n_blk), 1).astype(F32)
    turn = lax.broadcasted_iota(jnp.int32, (n_slot, 1), 0) % MOST

    def weights(pair, carry):
        plane = (n_plane * i - 1 + pair).astype(F32)
        here = meta_ref[0] == plane
        first = jnp.min(jnp.where(here, blk, 1e6), axis=1, keepdims=True)
        last = jnp.max(jnp.where(here, blk, -1.0), axis=1, keepdims=True)
        chosen = jnp.where(turn == 0, first, jnp.where(last > first, last, -2.0))
        mask = blk == chosen

        def pick(k):
            return jnp.sum(jnp.where(mask, meta_ref[k], 0.0), axis=1, keepdims=True)

        row, col, fz, fy = pick(1), pick(2), pick(3), pick(4)
        cols[pair] = jnp.broadcast_to(col, (n_slot, LANES))
        cosine, sine = wave(row * y * (1.0 / box))
        h_real = (1.0 - fy) + fy * step_cos
        h_imag = -fy * step_sin
        g_real = cosine * h_real + sine * h_imag
        g_imag = cosine * h_imag - sine * h_real
        for at, part in ((0, g_real), (n_slot, g_imag)):
            both = jnp.concatenate([part * (1.0 - fz), part * fz], axis=1)
            high, low = halves(both)
            g_high[pair, pl.ds(at, n_slot)] = high
            g_low[pair, pl.ds(at, n_slot)] = low
        return carry

    lax.fori_loop(0, n_pair, weights, 0)

    lane0 = lax.broadcasted_iota(jnp.int32, (n_slot, LANES), 1) == 0

    def evaluate(pair):
        rows = pl.ds(pl.multiple_of(pair * n_row, n_row), 2 * n_row)
        gh, gl = g_high[pair], g_low[pair]
        col = cols[pair]
        mirrored = col >= float(half_blocks)
        wanted = jnp.where(mirrored, 2.0 * half_blocks - 1.0 - col, col)
        wanted = wanted + jnp.where(mirrored & lane0, 1.0, 0.0)
        sign = jnp.where(mirrored, -1.0, 1.0)
        sign = jnp.where(lane0 & (wanted == 0.0), 0.0, sign)
        real = imag = None
        for cb in range(half_blocks):
            at = pl.ds(cb * 2 * LANES, 2 * LANES)
            zh, zl = z_high[rows, at], z_low[rows, at]
            prod = dot(gh, zh) + dot(gl, zh) + dot(gh, zl)
            a, b = prod[:n_slot, :LANES], prod[:n_slot, LANES:]
            c, d = prod[n_slot:, :LANES], prod[n_slot:, LANES:]
            if cb == 0:
                middle = wanted == float(half_blocks)
                real = jnp.where(middle, b, a - sign * d)
                imag = jnp.where(middle, d, c + sign * b)
            else:
                match = wanted == float(cb)
                real = jnp.where(match, a - sign * d, real)
                imag = jnp.where(match, c + sign * b, imag)
        stage[pair, :, pl.ds(0, LANES)] = real
        stage[pair, :, pl.ds(LANES, LANES)] = imag

    def sends(pair):
        copies = []
        for d in range(1, n_slab):
            to = lax.rem(s + d, n_slab)
            copies.append(
                pltpu.make_async_remote_copy(
                    src_ref=stage.at[pair, pl.ds(pl.multiple_of(to * tile, tile), tile)],
                    dst_ref=recv.at[pair, d - 1],
                    send_sem=send_sem.at[pair],
                    recv_sem=recv_sem.at[pair],
                    device_id=(to, i),
                    device_id_type=MESH,
                )
            )
        return copies

    def transform(step):
        for k in range(per_step):
            vol_copy(step * per_step + k).wait()
        x = vol[pl.ds(step * per_step, per_step)].reshape(per_step * n_row, box)
        xh, xl = halves(x)
        rows = pl.ds(pl.multiple_of((step * per_step + 1) * n_row, n_row), per_step * n_row)
        for cb in range(half_blocks):
            at = pl.ds(cb * 2 * LANES, 2 * LANES)
            th, tl = t_high[:, at], t_low[:, at]
            z = dot(xh, th) + dot(xl, th) + dot(xh, tl)
            zh, zl = halves(z)
            z_high[rows, at] = zh
            z_low[rows, at] = zl

    for copy in tab_copies:
        copy.wait()
    pl.semaphore_wait(barrier, n_slab - 1 + n_img - 1)

    def body(step, carry):
        transform(step)
        for k in range(per_step):
            pair = step * per_step + k
            evaluate(pair)
            for copy in sends(pair):
                copy.start()
        return carry

    lax.fori_loop(0, n_plane // per_step, body, 0)
    evaluate(n_plane)
    for copy in sends(n_plane):
        copy.start()

    own = pl.ds(pl.multiple_of(s * tile, tile), tile)
    for pair in range(n_pair):
        pltpu.make_async_copy(recv.at[pair], recv.at[pair], recv_sem.at[pair]).wait()
        total = stage[pair, own]
        for d in range(n_slab - 1):
            total = total + recv[pair, d]
        for to in range(n_img):
            red[to, pl.ds(MOST * pair, MOST)] = total[MOST * to : MOST * to + MOST]

    copies = []
    for d in range(1, n_img):
        to = lax.rem(i + d, n_img)
        copies.append(
            pltpu.make_async_remote_copy(
                src_ref=red.at[to],
                dst_ref=recv2.at[i],
                send_sem=send2_sem.at[d - 1],
                recv_sem=recv2_sem.at[d - 1],
                device_id=(s, to),
                device_id_type=MESH,
            )
        )
    for copy in copies:
        copy.start()
    recv2[i] = red[i]

    group = s * n_img + i
    eye = lax.broadcasted_iota(jnp.int32, (n_blk, n_blk), 0) == lax.broadcasted_iota(jnp.int32, (n_blk, n_blk), 1)
    before = lax.broadcasted_iota(jnp.int32, (n_blk, n_blk), 1) < lax.broadcasted_iota(jnp.int32, (n_blk, n_blk), 0)
    lines = [meta_ref[k, pl.ds(group * MOST, 1)] for k in range(6)]
    plane_b, row_b, col_b, _, _, focus_b = [
        jnp.sum(jnp.where(eye, v, 0.0), axis=1, keepdims=True) for v in lines
    ]
    rank_b = jnp.sum(jnp.where(before & (lines[0] == plane_b), 1.0, 0.0), axis=1, keepdims=True)
    pad = red.shape[1]
    n_sum = n_img * pad
    place = lax.broadcasted_iota(jnp.int32, (n_blk, n_sum), 1)
    img_of = jnp.zeros_like(place)
    for k in range(1, n_img):
        img_of = img_of + jnp.where(place >= k * pad, 1, 0)
    rest = place - img_of * pad
    plane_of = (img_of * n_plane - 1 + rest // MOST).astype(F32)
    turn_of = (rest % MOST).astype(F32)
    take = (rest < MOST * n_pair) & (plane_of == plane_b) & (turn_of == rank_b)
    take = jnp.where(take, 1.0, 0.0).astype(BF16)

    lane_x = lax.broadcasted_iota(jnp.int32, (n_blk, LANES), 1).astype(F32)
    column_x = col_b * LANES + lane_x
    fold_x = jnp.minimum(column_x, box - column_x)
    fold_y = jnp.minimum(row_b, box - row_b)
    wave_sq = (fold_x * fold_x + fold_y * fold_y) * (1.0 / (box * box))
    ctf = -jnp.sin(CTF_SCALE * focus_b * wave_sq + CTF_PHASE) * (1.0 / box)
    turned = (
        lax.broadcasted_iota(jnp.int32, (LANES, LANES), 0) + lax.broadcasted_iota(jnp.int32, (LANES, LANES), 1)
    ) % LANES == 0
    turned = jnp.where(turned, 1.0, 0.0).astype(BF16)
    mirrored_b = col_b >= float(half_blocks)

    for copy in copies:
        copy.wait_recv()
    all_high, all_low = halves(recv2[...].reshape(n_sum, 2 * LANES))
    value = dot(take, all_high) + dot(take, all_low)
    for k in range(2):
        part = value[:, k * LANES : (k + 1) * LANES]
        high, low = halves(part)
        back = dot(high, turned) + dot(low, turned)
        out_ref[:, k, :] = jnp.where(mirrored_b, back, part) * ctf

    for copy in copies:
        copy.wait_send()
    for pair in range(n_pair):
        some = stage.at[pair, pl.ds(0, (n_slab - 1) * tile)]
        pltpu.make_async_copy(some, some, send_sem.at[pair]).wait()


def on_device(n_slab, n_img, volume, blk_plane, blk_row, blk_col, frac_plane, frac_row, defocus):
    n_plane, n_row, box = volume.shape
    n_image, img_blk = blk_plane.shape
    n_group = n_slab * n_img
    n_blk = n_image // n_group * img_blk
    n_pair = n_plane + 1
    n_slot = MOST * n_group
    tile = MOST * n_img
    per_step = 2
    pad = -(-MOST * n_pair // 8) * 8
    focus = jnp.broadcast_to(defocus[:, None], blk_plane.shape)
    meta = jnp.stack(
        [v.astype(F32) for v in (blk_plane, blk_row, blk_col, frac_plane, frac_row, focus)]
    ).reshape(6, n_group, 1, n_blk)
    meta = jnp.broadcast_to(meta, (6, n_group, MOST, n_blk)).reshape(6, n_slot, n_blk)
    table_high, table_low = column_table(box)
    dims = (n_slab, n_img, n_plane, n_row, box, n_group, n_blk, per_step)
    any_space = pl.BlockSpec(memory_space=pl.ANY)
    vmem = pl.BlockSpec(memory_space=pltpu.VMEM)
    out = pl.pallas_call(
        functools.partial(kernel, dims),
        out_shape=jax.ShapeDtypeStruct((n_blk, 2, LANES), F32),
        in_specs=[vmem, any_space, any_space, any_space],
        out_specs=vmem,
        scratch_shapes=[
            pltpu.VMEM((n_plane, n_row, box), F32),
            pltpu.VMEM((box, box), BF16),
            pltpu.VMEM((box, box), BF16),
            pltpu.VMEM(((n_plane + 2) * n_row, box), BF16),
            pltpu.VMEM(((n_plane + 2) * n_row, box), BF16),
            pltpu.VMEM((n_pair, 2 * n_slot, 2 * n_row), BF16),
            pltpu.VMEM((n_pair, 2 * n_slot, 2 * n_row), BF16),
            pltpu.VMEM((n_pair, n_slot, LANES), F32),
            pltpu.VMEM((n_pair, n_slot, 2 * LANES), F32),
            pltpu.VMEM((n_pair, n_slab - 1, tile, 2 * LANES), F32),
            pltpu.VMEM((n_img, pad, 2 * LANES), F32),
            pltpu.VMEM((n_img, pad, 2 * LANES), F32),
            pltpu.SemaphoreType.DMA((n_plane,)),
            pltpu.SemaphoreType.DMA((2,)),
            pltpu.SemaphoreType.DMA((n_pair,)),
            pltpu.SemaphoreType.DMA((n_pair,)),
            pltpu.SemaphoreType.DMA((n_img - 1,)),
            pltpu.SemaphoreType.DMA((n_img - 1,)),
        ],
        compiler_params=pltpu.CompilerParams(
            collective_id=0, has_side_effects=True, vmem_limit_bytes=58 * 1024 * 1024
        ),
        cost_estimate=pl.CostEstimate(flops=8_000_000_000, bytes_accessed=9_000_000, transcendentals=0),
        name="slices",
    )(meta, volume, jnp.asarray(table_high), jnp.asarray(table_low))
    return out.reshape(n_image // n_group, img_blk, 2, LANES)


def solution(mesh):
    placed = (P("img", "slab", None), P(), P(), P(), P(), P(), P())
    return jax.shard_map(
        functools.partial(on_device, mesh.shape["slab"], mesh.shape["img"]),
        mesh=mesh,
        in_specs=placed,
        out_specs=P(("slab", "img"), None, None, None),
        check_vma=False,
    )
```

```python
import functools
import math

import jax
import jax.numpy as jnp
import ml_dtypes
import numpy as np
from jax import lax
from jax.experimental import pallas as pl
from jax.experimental.pallas import tpu as pltpu
from jax.sharding import PartitionSpec as P

LANES = 128
CTF_SCALE = 20.0
CTF_PHASE = 0.07
MOST = 2
MESH = pl.DeviceIdType.MESH
F32 = jnp.float32
BF16 = jnp.bfloat16


def wave_coefficients():
    grid = 0.5 * np.cos(np.linspace(0.0, np.pi, 4001))
    grid = grid[grid > 1e-6]
    basis = (4 * grid * grid)[:, None] ** np.arange(8)
    scale = 4.0 ** np.arange(8)
    cos_c = np.linalg.lstsq(basis, np.cos(2 * np.pi * grid), rcond=None)[0] * scale
    sin_c = np.linalg.lstsq(basis[:, :7] * grid[:, None], np.sin(2 * np.pi * grid), rcond=None)[0] * scale[:7]
    return [float(v) for v in cos_c], [float(v) for v in sin_c]


COS_C, SIN_C = wave_coefficients()


def horner(coefficients, value):
    total = jnp.full_like(value, coefficients[-1])
    for c in coefficients[-2::-1]:
        total = total * value + c
    return total


def wave(turns):
    part = turns - jnp.round(turns)
    square = part * part
    return horner(COS_C, square), part * horner(SIN_C, square)


def split_table(table):
    high = table.astype(ml_dtypes.bfloat16)
    low = (table - high.astype(np.float64)).astype(ml_dtypes.bfloat16)
    return high, low


def column_table(box):
    half, lower = box // 2, LANES // 2
    lane = np.arange(LANES)
    parts = []
    for u in range(half // LANES // 2):
        first = 2 * u * LANES
        even = first + 2 * lane
        odd = first + np.where(lane < lower, LANES + 2 * lane + 1, 2 * (lane - lower) + 1)
        for wanted in (even, odd):
            angle = ((np.arange(half)[:, None] * wanted[None, :]) % box) * (2.0 * np.pi / box)
            real, imag = np.cos(angle), -np.sin(angle)
            imag[:, wanted == 0] = (1.0 - 2.0 * (np.arange(half) % 2))[:, None]
            parts += [real, imag]
    return split_table(np.concatenate(parts, axis=1))


def halves(value):
    high = value.astype(BF16)
    low = (value - high.astype(F32)).astype(BF16)
    return high, low


def dot(a, b):
    return jnp.dot(a, b, preferred_element_type=F32)


def kernel(
    dims, plane_hbm, row_hbm, col_hbm, fz_hbm, fy_hbm, focus_hbm, vol_hbm, high_hbm, low_hbm, out_ref,
    ints, floats, focus_ref, meta_ref, vol, t_high, t_low, z_high, z_low, stage, recv, red, recv2,
    meta_sem, vol_sem, tab_sem, send_sem, recv_sem, send2_sem, recv2_sem,
):
    n_slab, n_img, n_plane, n_row, box, n_group, n_blk, per_step = dims
    n_pair = n_plane + 1
    n_slot = MOST * n_group
    tile = MOST * n_img
    half_blocks = box // LANES // 2
    lower = LANES // 2
    s, i = lax.axis_index("slab"), lax.axis_index("img")

    meta_copies = [
        pltpu.make_async_copy(source, target, meta_sem.at[k])
        for k, (source, target) in enumerate(
            [
                (plane_hbm, ints.at[0]), (row_hbm, ints.at[1]), (col_hbm, ints.at[2]),
                (fz_hbm, floats.at[0]), (fy_hbm, floats.at[1]), (focus_hbm, focus_ref),
            ]
        )
    ]
    tab_copies = [
        pltpu.make_async_copy(high_hbm, t_high, tab_sem.at[0]),
        pltpu.make_async_copy(low_hbm, t_low, tab_sem.at[1]),
    ]

    def vol_copy(q):
        return pltpu.make_async_copy(vol_hbm.at[q], vol.at[q], vol_sem.at[q])

    for copy in meta_copies:
        copy.start()
    tab_copies[0].start()
    for q in range(per_step):
        vol_copy(q).start()
    tab_copies[1].start()
    for q in range(per_step, n_plane):
        vol_copy(q).start()

    barrier = pltpu.get_barrier_semaphore()
    for d in range(1, n_slab):
        pl.semaphore_signal(barrier, inc=1, device_id=(lax.rem(s + d, n_slab), i), device_id_type=MESH)
    for d in range(1, n_img):
        pl.semaphore_signal(barrier, inc=1, device_id=(s, lax.rem(i + d, n_img)), device_id_type=MESH)

    zero_rows = jnp.zeros((n_row, box), BF16)
    for ref in (z_high, z_low):
        ref[pl.ds(0, n_row)] = zero_rows
        ref[pl.ds((n_plane + 1) * n_row, n_row)] = zero_rows
    red[...] = jnp.zeros_like(red)

    for copy in meta_copies:
        copy.wait()
    img_blk, n_image = ints.shape[1:]
    own_images = n_image // n_group
    image = lax.broadcasted_iota(jnp.int32, (n_blk, n_image), 1)
    within = lax.broadcasted_iota(jnp.int32, (n_blk, n_image), 0) // img_blk
    in_turn = image % own_images == within
    slot_at = lax.broadcasted_iota(jnp.int32, (n_slot, n_image), 0) // MOST
    image_at = lax.broadcasted_iota(jnp.int32, (n_slot, n_image), 1) // own_images
    spread = jnp.where(slot_at == image_at, 1.0, 0.0)
    sources = [ints[k].astype(F32) for k in range(3)] + [floats[0], floats[1]]
    sources.append(jnp.broadcast_to(focus_ref[...], (img_blk, n_image)))
    for k, source in enumerate(sources):
        laid = jnp.where(in_turn, jnp.concatenate([source] * own_images, axis=0), 0.0)
        meta_ref[k] = lax.dot_general(
            spread, laid, (((1,), (1,)), ((), ())),
            precision=lax.Precision.HIGHEST, preferred_element_type=F32,
        )

    lane = lax.broadcasted_iota(jnp.int32, (1, n_row), 1)
    y = (lane + s * n_row).astype(F32)
    step_cos, step_sin = wave(y * (1.0 / box))
    blk = lax.broadcasted_iota(jnp.int32, (n_slot, n_blk), 1).astype(F32)
    turn = lax.broadcasted_iota(jnp.int32, (n_slot, 1), 0) % MOST

    def weights(pair):
        plane = (n_plane * i - 1 + pair).astype(F32)
        here = meta_ref[0] == plane
        first = jnp.min(jnp.where(here, blk, 1e6), axis=1, keepdims=True)
        last = jnp.max(jnp.where(here, blk, -1.0), axis=1, keepdims=True)
        chosen = jnp.where(turn == 0, first, jnp.where(last > first, last, -2.0))
        mask = blk == chosen

        def pick(k):
            return jnp.sum(jnp.where(mask, meta_ref[k], 0.0), axis=1, keepdims=True)

        row, col, fz, fy = pick(1), pick(2), pick(3), pick(4)
        cosine, sine = wave(row * y * (1.0 / box))
        h_real = (1.0 - fy) + fy * step_cos
        h_imag = -fy * step_sin
        g_real = cosine * h_real + sine * h_imag
        g_imag = cosine * h_imag - sine * h_real
        both = [jnp.concatenate([part * (1.0 - fz), part * fz], axis=1) for part in (g_real, g_imag)]
        high, low = halves(jnp.concatenate(both, axis=0))
        return col, high, low

    slot_lane = lax.broadcasted_iota(jnp.int32, (n_slot, LANES), 1)

    def evaluate(pair, given):
        rows = pl.ds(pair * n_row, 2 * n_row)
        if not isinstance(pair, int):
            rows = pl.ds(pl.multiple_of(pair * n_row, n_row), 2 * n_row)
        col, gh, gl = given
        mirrored = col >= float(half_blocks)
        base = jnp.where(mirrored, 2.0 * half_blocks - 1.0 - col, col)
        odd = base - 2.0 * jnp.floor(base * 0.5)
        wanted = jnp.where(slot_lane < lower, base, base + 1.0 - 2.0 * odd)
        sign = jnp.where(mirrored, -1.0, 1.0)
        sign = jnp.where((slot_lane == 0) & (wanted == 0.0), 0.0, sign)
        beyond = jnp.where(base == half_blocks - 1.0, -1.0, base + odd)
        beyond = jnp.broadcast_to(beyond, (n_slot, LANES))
        real = imag = past_real = past_imag = None
        for cb in range(half_blocks):
            at = pl.ds(cb * 2 * LANES, 2 * LANES)
            zh, zl = z_high[rows, at], z_low[rows, at]
            prod = dot(gh, zh) + dot(gl, zh) + dot(gh, zl)
            a, b = prod[:n_slot, :LANES], prod[:n_slot, LANES:]
            c, d = prod[n_slot:, :LANES], prod[n_slot:, LANES:]
            now_real, now_imag = a - sign * d, c + sign * b
            if cb == 0:
                real, imag = now_real, now_imag
                middle = beyond == -1.0
                past_real = jnp.where(middle, b, now_real)
                past_imag = jnp.where(middle, d, now_imag)
            else:
                match = wanted == float(cb)
                real = jnp.where(match, now_real, real)
                imag = jnp.where(match, now_imag, imag)
                if cb % 2 == 0:
                    match = beyond == float(cb)
                    past_real = jnp.where(match, now_real, past_real)
                    past_imag = jnp.where(match, now_imag, past_imag)
        put = mirrored & (slot_lane == jnp.where(odd > 0.0, lower, 0))
        stage[pair, :, pl.ds(0, LANES)] = jnp.where(put, pltpu.roll(past_real, lower, 1), real)
        stage[pair, :, pl.ds(LANES, LANES)] = jnp.where(put, pltpu.roll(past_imag, lower, 1), imag)

    def sends(pair):
        copies = []
        for d in range(1, n_slab):
            to = lax.rem(s + d, n_slab)
            copies.append(
                pltpu.make_async_remote_copy(
                    src_ref=stage.at[pair, pl.ds(pl.multiple_of(to * tile, tile), tile)],
                    dst_ref=recv.at[pair, d - 1],
                    send_sem=send_sem.at[pair],
                    recv_sem=recv_sem.at[pair],
                    device_id=(to, i),
                    device_id_type=MESH,
                )
            )
        return copies

    def transform(step):
        for k in range(per_step):
            vol_copy(step * per_step + k).wait()
        planes = pl.ds(step * per_step, per_step)
        near = vol[planes, :, pl.ds(0, box // 2)].reshape(per_step * n_row, box // 2)
        far = vol[planes, :, pl.ds(box // 2, box // 2)].reshape(per_step * n_row, box // 2)
        inputs = (halves(near + far), halves(near - far))
        if step == 0:
            for copy in tab_copies:
                copy.wait()
        rows = pl.ds((step * per_step + 1) * n_row, per_step * n_row)
        for cb in range(half_blocks):
            xh, xl = inputs[cb % 2]
            at = pl.ds(cb * 2 * LANES, 2 * LANES)
            th, tl = t_high[:, at], t_low[:, at]
            z = dot(xh, th) + dot(xl, th) + dot(xh, tl)
            zh, zl = halves(z)
            z_high[rows, at] = zh
            z_low[rows, at] = zl

    for step in range(n_plane // per_step):
        if per_step <= 2:
            given = [weights(step * per_step + k) for k in range(per_step)]
            transform(step)
            if step == 0:
                pl.semaphore_wait(barrier, n_slab - 1 + n_img - 1)
            for k in range(per_step):
                pair = step * per_step + k
                evaluate(pair, given[k])
                for copy in sends(pair):
                    copy.start()
        else:
            transform(step)
            if step == 0:
                pl.semaphore_wait(barrier, n_slab - 1 + n_img - 1)

            def body(k, carry):
                evaluate(k, weights(k))
                for copy in sends(k):
                    copy.start()
                return carry

            lax.fori_loop(step * per_step, (step + 1) * per_step, body, 0)
    evaluate(n_plane, weights(n_plane))
    for copy in sends(n_plane):
        copy.start()

    own = pl.ds(pl.multiple_of(s * tile, tile), tile)
    for pair in range(n_pair):
        pltpu.make_async_copy(recv.at[pair], recv.at[pair], recv_sem.at[pair]).wait()
        total = stage[pair, own]
        for d in range(n_slab - 1):
            total = total + recv[pair, d]
        for to in range(n_img):
            red[to, pl.ds(MOST * pair, MOST)] = total[MOST * to : MOST * to + MOST]

    copies = []
    for d in range(1, n_img):
        to = lax.rem(i + d, n_img)
        copies.append(
            pltpu.make_async_remote_copy(
                src_ref=red.at[to],
                dst_ref=recv2.at[i],
                send_sem=send2_sem.at[d - 1],
                recv_sem=recv2_sem.at[d - 1],
                device_id=(s, to),
                device_id_type=MESH,
            )
        )
    for copy in copies:
        copy.start()
    recv2[i] = red[i]

    group = s * n_img + i
    eye = lax.broadcasted_iota(jnp.int32, (n_blk, n_blk), 0) == lax.broadcasted_iota(jnp.int32, (n_blk, n_blk), 1)
    before = lax.broadcasted_iota(jnp.int32, (n_blk, n_blk), 1) < lax.broadcasted_iota(jnp.int32, (n_blk, n_blk), 0)
    lines = [meta_ref[k, pl.ds(group * MOST, 1)] for k in range(6)]
    plane_b, row_b, col_b, _, _, focus_b = [
        jnp.sum(jnp.where(eye, v, 0.0), axis=1, keepdims=True) for v in lines
    ]
    rank_b = jnp.sum(jnp.where(before & (lines[0] == plane_b), 1.0, 0.0), axis=1, keepdims=True)
    pad = red.shape[1]
    n_sum = n_img * pad
    place = lax.broadcasted_iota(jnp.int32, (n_blk, n_sum), 1)
    img_of = jnp.zeros_like(place)
    for k in range(1, n_img):
        img_of = img_of + jnp.where(place >= k * pad, 1, 0)
    rest = place - img_of * pad
    plane_of = (img_of * n_plane - 1 + rest // MOST).astype(F32)
    turn_of = (rest % MOST).astype(F32)
    take = (rest < MOST * n_pair) & (plane_of == plane_b) & (turn_of == rank_b)
    take = jnp.where(take, 1.0, 0.0).astype(BF16)

    lane_x = lax.broadcasted_iota(jnp.int32, (n_blk, LANES), 1).astype(F32)
    column_x = col_b * LANES + lane_x
    fold_x = jnp.minimum(column_x, box - column_x)
    fold_y = jnp.minimum(row_b, box - row_b)
    wave_sq = (fold_x * fold_x + fold_y * fold_y) * (1.0 / (box * box))
    ctf = -jnp.sin(CTF_SCALE * focus_b * wave_sq + CTF_PHASE) * (1.0 / box)
    source_lane = lax.broadcasted_iota(jnp.int32, (LANES, LANES), 0)
    target_lane = lax.broadcasted_iota(jnp.int32, (LANES, LANES), 1)
    low_half = source_lane < lower
    orders = []
    for offset in (
        jnp.where(low_half, 2 * source_lane, 2 * source_lane - LANES + 1),
        jnp.where(low_half, 2 * source_lane + 1, 2 * source_lane - LANES),
    ):
        orders.append(offset == target_lane)
        orders.append((offset + target_lane) % LANES == 0)
    orders = jnp.concatenate([jnp.where(v, 1.0, 0.0).astype(BF16) for v in orders], axis=1)
    mirrored_b = col_b >= float(half_blocks)
    base_b = jnp.where(mirrored_b, 2.0 * half_blocks - 1.0 - col_b, col_b)
    odd_b = base_b - 2.0 * jnp.floor(base_b * 0.5) > 0.0

    for copy in copies:
        copy.wait_recv()
    all_high, all_low = halves(recv2[...].reshape(n_sum, 2 * LANES))
    value = dot(take, all_high) + dot(take, all_low)
    for k in range(2):
        part = value[:, k * LANES : (k + 1) * LANES]
        high, low = halves(part)
        laid = dot(high, orders) + dot(low, orders)
        laid = [laid[:, v * LANES : (v + 1) * LANES] for v in range(4)]
        even = jnp.where(mirrored_b, laid[1], laid[0])
        odd = jnp.where(mirrored_b, laid[3], laid[2])
        out_ref[:, k, :] = jnp.where(odd_b, odd, even) * ctf

    for copy in copies:
        copy.wait_send()
    for pair in range(n_pair):
        some = stage.at[pair, pl.ds(0, (n_slab - 1) * tile)]
        pltpu.make_async_copy(some, some, send_sem.at[pair]).wait()


def on_device(n_slab, n_img, volume, blk_plane, blk_row, blk_col, frac_plane, frac_row, defocus):
    n_plane, n_row, box = volume.shape
    n_image, img_blk = blk_plane.shape
    n_group = n_slab * n_img
    n_blk = n_image // n_group * img_blk
    n_pair = n_plane + 1
    n_slot = MOST * n_group
    tile = MOST * n_img
    per_step = max(1, min(n_plane, 256 // n_row))
    pad = -(-MOST * n_pair // 8) * 8
    table_high, table_low = column_table(box)
    dims = (n_slab, n_img, n_plane, n_row, box, n_group, n_blk, per_step)
    any_space = pl.BlockSpec(memory_space=pl.ANY)
    vmem = pl.BlockSpec(memory_space=pltpu.VMEM)
    out = pl.pallas_call(
        functools.partial(kernel, dims),
        out_shape=jax.ShapeDtypeStruct((n_blk, 2, LANES), F32),
        in_specs=[any_space] * 9,
        out_specs=vmem,
        scratch_shapes=[
            pltpu.VMEM((3, img_blk, n_image), jnp.int32),
            pltpu.VMEM((2, img_blk, n_image), F32),
            pltpu.VMEM((1, n_image), F32),
            pltpu.VMEM((6, n_slot, n_blk), F32),
            pltpu.VMEM((n_plane, n_row, box), F32),
            pltpu.VMEM((box // 2, box), BF16),
            pltpu.VMEM((box // 2, box), BF16),
            pltpu.VMEM(((n_plane + 2) * n_row, box), BF16),
            pltpu.VMEM(((n_plane + 2) * n_row, box), BF16),
            pltpu.VMEM((n_pair, n_slot, 2 * LANES), F32),
            pltpu.VMEM((n_pair, n_slab - 1, tile, 2 * LANES), F32),
            pltpu.VMEM((n_img, pad, 2 * LANES), F32),
            pltpu.VMEM((n_img, pad, 2 * LANES), F32),
            pltpu.SemaphoreType.DMA((6,)),
            pltpu.SemaphoreType.DMA((n_plane,)),
            pltpu.SemaphoreType.DMA((2,)),
            pltpu.SemaphoreType.DMA((n_pair,)),
            pltpu.SemaphoreType.DMA((n_pair,)),
            pltpu.SemaphoreType.DMA((n_img - 1,)),
            pltpu.SemaphoreType.DMA((n_img - 1,)),
        ],
        compiler_params=pltpu.CompilerParams(
            collective_id=0, has_side_effects=True, vmem_limit_bytes=58 * 1024 * 1024
        ),
        cost_estimate=pl.CostEstimate(flops=8_000_000_000, bytes_accessed=9_000_000, transcendentals=0),
        name="slices",
    )(
        blk_plane.T, blk_row.T, blk_col.T, frac_plane.T, frac_row.T, defocus[None, :],
        volume, jnp.asarray(table_high), jnp.asarray(table_low),
    )
    return out.reshape(n_image // n_group, img_blk, 2, LANES)


def solution(mesh):
    placed = (P("img", "slab", None), P(), P(), P(), P(), P(), P())
    return jax.shard_map(
        functools.partial(on_device, mesh.shape["slab"], mesh.shape["img"]),
        mesh=mesh,
        in_specs=placed,
        out_specs=P(("slab", "img"), None, None, None),
        check_vma=False,
    )
```

```python
import functools
import math

import jax
import jax.numpy as jnp
import ml_dtypes
import numpy as np
from jax import lax
from jax.experimental import pallas as pl
from jax.experimental.pallas import tpu as pltpu
from jax.sharding import PartitionSpec as P

LANES = 128
CTF_SCALE = 20.0
CTF_PHASE = 0.07
MOST = 2
CORES = 2
MESH = pl.DeviceIdType.MESH
F32 = jnp.float32
BF16 = jnp.bfloat16


def wave_coefficients():
    grid = 0.5 * np.cos(np.linspace(0.0, np.pi, 4001))
    grid = grid[grid > 1e-6]
    basis = (4 * grid * grid)[:, None] ** np.arange(8)
    scale = 4.0 ** np.arange(8)
    cos_c = np.linalg.lstsq(basis, np.cos(2 * np.pi * grid), rcond=None)[0] * scale
    sin_c = np.linalg.lstsq(basis[:, :7] * grid[:, None], np.sin(2 * np.pi * grid), rcond=None)[0] * scale[:7]
    return [float(v) for v in cos_c], [float(v) for v in sin_c]


COS_C, SIN_C = wave_coefficients()


def horner(coefficients, value):
    total = jnp.full_like(value, coefficients[-1])
    for c in coefficients[-2::-1]:
        total = total * value + c
    return total


def wave(turns):
    part = turns - jnp.round(turns)
    square = part * part
    return horner(COS_C, square), part * horner(SIN_C, square)


def split_table(table):
    high = table.astype(ml_dtypes.bfloat16)
    low = (table - high.astype(np.float64)).astype(ml_dtypes.bfloat16)
    return high, low


def column_table(box):
    half, lower = box // 2, LANES // 2
    lane = np.arange(LANES)
    parts = []
    for u in range(half // LANES // 2):
        first = 2 * u * LANES
        even = first + 2 * lane
        odd = first + np.where(lane < lower, LANES + 2 * lane + 1, 2 * (lane - lower) + 1)
        for wanted in (even, odd):
            angle = ((np.arange(half)[:, None] * wanted[None, :]) % box) * (2.0 * np.pi / box)
            real, imag = np.cos(angle), -np.sin(angle)
            imag[:, wanted == 0] = (1.0 - 2.0 * (np.arange(half) % 2))[:, None]
            parts += [real, imag]
    return split_table(np.concatenate(parts, axis=1))


def halves(value):
    high = value.astype(BF16)
    low = (value - high.astype(F32)).astype(BF16)
    return high, low


def dot(a, b):
    return jnp.dot(a, b, preferred_element_type=F32)


def kernel(
    dims, plane_hbm, row_hbm, col_hbm, fz_hbm, fy_hbm, focus_hbm, vol_hbm, high_hbm, low_hbm, out_ref,
    ints, floats, focus_ref, meta_ref, vol, t_high, t_low, z_high, z_low, stage, recv_twin, joined, recv, red, recv2,
    meta_sem, vol_sem, tab_sem, twin_sem, send_sem, recv_sem, send2_sem, recv2_sem,
):
    n_slab, n_img, n_plane, n_row, box, n_group, n_blk, per_step = dims
    n_pair = n_plane + 1
    n_slot = MOST * n_group
    tile = MOST * n_img
    half_blocks = box // LANES // 2
    lower = LANES // 2
    n_chip = n_slab // CORES
    half_slots = n_slot // CORES
    s, i = lax.axis_index("slab"), lax.axis_index("img")
    chip, core = s // CORES, s % CORES
    twin = chip * CORES + 1 - core

    meta_copies = [
        pltpu.make_async_copy(source, target, meta_sem.at[k])
        for k, (source, target) in enumerate(
            [
                (plane_hbm, ints.at[0]), (row_hbm, ints.at[1]), (col_hbm, ints.at[2]),
                (fz_hbm, floats.at[0]), (fy_hbm, floats.at[1]), (focus_hbm, focus_ref),
            ]
        )
    ]
    tab_copies = [
        pltpu.make_async_copy(high_hbm, t_high, tab_sem.at[0]),
        pltpu.make_async_copy(low_hbm, t_low, tab_sem.at[1]),
    ]

    def vol_copy(q):
        return pltpu.make_async_copy(vol_hbm.at[q], vol.at[q], vol_sem.at[q])

    for copy in meta_copies:
        copy.start()
    tab_copies[0].start()
    for q in range(per_step):
        vol_copy(q).start()
    tab_copies[1].start()
    for q in range(per_step, n_plane):
        vol_copy(q).start()

    barrier = pltpu.get_barrier_semaphore()
    pl.semaphore_signal(barrier, inc=1, device_id=(twin, i), device_id_type=MESH)
    for d in range(1, n_chip):
        to = lax.rem(chip + d, n_chip) * CORES + core
        pl.semaphore_signal(barrier, inc=1, device_id=(to, i), device_id_type=MESH)
    for d in range(1, n_img):
        pl.semaphore_signal(barrier, inc=1, device_id=(s, lax.rem(i + d, n_img)), device_id_type=MESH)

    zero_rows = jnp.zeros((n_row, box), BF16)
    for ref in (z_high, z_low):
        ref[pl.ds(0, n_row)] = zero_rows
        ref[pl.ds((n_plane + 1) * n_row, n_row)] = zero_rows
    red[...] = jnp.zeros_like(red)

    for copy in meta_copies:
        copy.wait()
    img_blk, n_image = ints.shape[1:]
    own_images = n_image // n_group
    image = lax.broadcasted_iota(jnp.int32, (n_blk, n_image), 1)
    within = lax.broadcasted_iota(jnp.int32, (n_blk, n_image), 0) // img_blk
    in_turn = image % own_images == within
    slot_at = lax.broadcasted_iota(jnp.int32, (n_slot, n_image), 0)
    slot_core = jnp.where(slot_at >= half_slots, 1, 0)
    slot_at = slot_at - slot_core * half_slots
    slot_at = (slot_at // tile * CORES + slot_core) * n_img + slot_at % tile // MOST
    image_at = lax.broadcasted_iota(jnp.int32, (n_slot, n_image), 1) // own_images
    spread = jnp.where(slot_at == image_at, 1.0, 0.0)
    sources = [ints[k].astype(F32) for k in range(3)] + [floats[0], floats[1]]
    sources.append(jnp.broadcast_to(focus_ref[...], (img_blk, n_image)))
    for k, source in enumerate(sources):
        laid = jnp.where(in_turn, jnp.concatenate([source] * own_images, axis=0), 0.0)
        meta_ref[k] = lax.dot_general(
            spread, laid, (((1,), (1,)), ((), ())),
            precision=lax.Precision.HIGHEST, preferred_element_type=F32,
        )

    lane = lax.broadcasted_iota(jnp.int32, (1, n_row), 1)
    y = (lane + s * n_row).astype(F32)
    step_cos, step_sin = wave(y * (1.0 / box))
    blk = lax.broadcasted_iota(jnp.int32, (n_slot, n_blk), 1).astype(F32)
    turn = lax.broadcasted_iota(jnp.int32, (n_slot, 1), 0) % MOST

    def weights(pair):
        plane = (n_plane * i - 1 + pair).astype(F32)
        here = meta_ref[0] == plane
        first = jnp.min(jnp.where(here, blk, 1e6), axis=1, keepdims=True)
        last = jnp.max(jnp.where(here, blk, -1.0), axis=1, keepdims=True)
        chosen = jnp.where(turn == 0, first, jnp.where(last > first, last, -2.0))
        mask = blk == chosen

        def pick(k):
            return jnp.sum(jnp.where(mask, meta_ref[k], 0.0), axis=1, keepdims=True)

        row, col, fz, fy = pick(1), pick(2), pick(3), pick(4)
        cosine, sine = wave(row * y * (1.0 / box))
        h_real = (1.0 - fy) + fy * step_cos
        h_imag = -fy * step_sin
        g_real = cosine * h_real + sine * h_imag
        g_imag = cosine * h_imag - sine * h_real
        both = [jnp.concatenate([part * (1.0 - fz), part * fz], axis=1) for part in (g_real, g_imag)]
        high, low = halves(jnp.concatenate(both, axis=0))
        return col, high, low

    slot_lane = lax.broadcasted_iota(jnp.int32, (n_slot, LANES), 1)

    def evaluate(pair, given):
        rows = pl.ds(pair * n_row, 2 * n_row)
        if not isinstance(pair, int):
            rows = pl.ds(pl.multiple_of(pair * n_row, n_row), 2 * n_row)
        col, gh, gl = given
        mirrored = col >= float(half_blocks)
        base = jnp.where(mirrored, 2.0 * half_blocks - 1.0 - col, col)
        odd = base - 2.0 * jnp.floor(base * 0.5)
        wanted = jnp.where(slot_lane < lower, base, base + 1.0 - 2.0 * odd)
        sign = jnp.where(mirrored, -1.0, 1.0)
        sign = jnp.where((slot_lane == 0) & (wanted == 0.0), 0.0, sign)
        beyond = jnp.where(base == half_blocks - 1.0, -1.0, base + odd)
        beyond = jnp.broadcast_to(beyond, (n_slot, LANES))
        real = imag = past_real = past_imag = None
        for cb in range(half_blocks):
            at = pl.ds(cb * 2 * LANES, 2 * LANES)
            zh, zl = z_high[rows, at], z_low[rows, at]
            prod = dot(gh, zh) + dot(gl, zh) + dot(gh, zl)
            a, b = prod[:n_slot, :LANES], prod[:n_slot, LANES:]
            c, d = prod[n_slot:, :LANES], prod[n_slot:, LANES:]
            now_real, now_imag = a - sign * d, c + sign * b
            if cb == 0:
                real, imag = now_real, now_imag
                middle = beyond == -1.0
                past_real = jnp.where(middle, b, now_real)
                past_imag = jnp.where(middle, d, now_imag)
            else:
                match = wanted == float(cb)
                real = jnp.where(match, now_real, real)
                imag = jnp.where(match, now_imag, imag)
                if cb % 2 == 0:
                    match = beyond == float(cb)
                    past_real = jnp.where(match, now_real, past_real)
                    past_imag = jnp.where(match, now_imag, past_imag)
        put = mirrored & (slot_lane == jnp.where(odd > 0.0, lower, 0))
        stage[pair, :, pl.ds(0, LANES)] = jnp.where(put, pltpu.roll(past_real, lower, 1), real)
        stage[pair, :, pl.ds(LANES, LANES)] = jnp.where(put, pltpu.roll(past_imag, lower, 1), imag)

    n_step = n_plane // per_step
    spans = [(g * per_step, per_step) for g in range(n_step)]
    spans[-1] = (spans[-1][0], per_step + 1)
    own_half = pl.multiple_of(core * half_slots, half_slots)
    other_half = pl.multiple_of((1 - core) * half_slots, half_slots)

    def twin_copy(g):
        pairs = pl.ds(*spans[g])
        return pltpu.make_async_remote_copy(
            src_ref=stage.at[pairs, pl.ds(other_half, half_slots)],
            dst_ref=recv_twin.at[pairs],
            send_sem=twin_sem.at[0, g],
            recv_sem=twin_sem.at[1, g],
            device_id=(twin, i),
            device_id_type=MESH,
        )

    def chip_copies(g):
        pairs = pl.ds(*spans[g])
        copies = []
        for d in range(1, n_chip):
            to = lax.rem(chip + d, n_chip)
            copies.append(
                pltpu.make_async_remote_copy(
                    src_ref=joined.at[pairs, pl.ds(pl.multiple_of(to * tile, tile), tile)],
                    dst_ref=recv.at[d - 1, pairs],
                    send_sem=send_sem.at[g, d - 1],
                    recv_sem=recv_sem.at[g, d - 1],
                    device_id=(to * CORES + core, i),
                    device_id_type=MESH,
                )
            )
        return copies

    def join(g):
        pairs = pl.ds(*spans[g])
        twin_copy(g).wait_recv()
        joined[pairs] = stage[pairs, pl.ds(own_half, half_slots)] + recv_twin[pairs]
        for copy in chip_copies(g):
            copy.start()

    def load(step):
        for k in range(per_step):
            vol_copy(step * per_step + k).wait()
        planes = pl.ds(step * per_step, per_step)
        near = vol[planes, :, pl.ds(0, box // 2)].reshape(per_step * n_row, box // 2)
        far = vol[planes, :, pl.ds(box // 2, box // 2)].reshape(per_step * n_row, box // 2)
        return halves(near + far), halves(near - far)

    def transform(step, inputs, chunks):
        rows = pl.ds((step * per_step + 1) * n_row, per_step * n_row)
        for cb in chunks:
            xh, xl = inputs[cb % 2]
            at = pl.ds(cb * 2 * LANES, 2 * LANES)
            th, tl = t_high[:, at], t_low[:, at]
            z = dot(xh, th) + dot(xl, th) + dot(xh, tl)
            zh, zl = halves(z)
            z_high[rows, at] = zh
            z_low[rows, at] = zl

    for copy in tab_copies:
        copy.wait()
    given = None
    few = per_step <= 2
    for step in range(n_step + 1):
        if step < n_step:
            inputs = load(step)
        ready = []
        if few:
            for k in range(per_step):
                if step < n_step:
                    ready.append(weights(step * per_step + k))
                    each = half_blocks // per_step
                    transform(step, inputs, range(k * each, (k + 1) * each))
                if step > 0:
                    evaluate((step - 1) * per_step + k, given[k])
            if step == n_step - 1:
                ready.append(weights(n_plane))
            if step == n_step:
                evaluate(n_plane, given[per_step])
        else:
            if step < n_step:
                transform(step, inputs, range(half_blocks))
            if step > 0:

                def body(k, carry):
                    evaluate(k, weights(k))
                    return carry

                lax.fori_loop(spans[step - 1][0], sum(spans[step - 1]), body, 0)
        given = ready
        if step == 1:
            pl.semaphore_wait(barrier, n_chip + n_img - 1)
        if step > 0:
            twin_copy(step - 1).start()
        if step > 1:
            join(step - 2)
    join(n_step - 1)

    own = pl.ds(pl.multiple_of(chip * tile, tile), tile)
    for g in range(n_step):
        for copy in chip_copies(g):
            copy.wait_recv()
        for pair in range(spans[g][0], sum(spans[g])):
            total = joined[pair, own]
            for d in range(n_chip - 1):
                total = total + recv[d, pair]
            for to in range(n_img):
                red[to, pl.ds(MOST * pair, MOST)] = total[MOST * to : MOST * to + MOST]

    copies = []
    for d in range(1, n_img):
        to = lax.rem(i + d, n_img)
        copies.append(
            pltpu.make_async_remote_copy(
                src_ref=red.at[to],
                dst_ref=recv2.at[i],
                send_sem=send2_sem.at[d - 1],
                recv_sem=recv2_sem.at[d - 1],
                device_id=(s, to),
                device_id_type=MESH,
            )
        )
    for copy in copies:
        copy.start()
    recv2[i] = red[i]

    group = s * n_img + i
    eye = lax.broadcasted_iota(jnp.int32, (n_blk, n_blk), 0) == lax.broadcasted_iota(jnp.int32, (n_blk, n_blk), 1)
    before = lax.broadcasted_iota(jnp.int32, (n_blk, n_blk), 1) < lax.broadcasted_iota(jnp.int32, (n_blk, n_blk), 0)
    own_line = core * half_slots + chip * tile + i * MOST
    lines = [meta_ref[k, pl.ds(own_line, 1)] for k in range(6)]
    plane_b, row_b, col_b, _, _, focus_b = [
        jnp.sum(jnp.where(eye, v, 0.0), axis=1, keepdims=True) for v in lines
    ]
    rank_b = jnp.sum(jnp.where(before & (lines[0] == plane_b), 1.0, 0.0), axis=1, keepdims=True)
    pad = red.shape[1]
    n_sum = n_img * pad
    place = lax.broadcasted_iota(jnp.int32, (n_blk, n_sum), 1)
    img_of = jnp.zeros_like(place)
    for k in range(1, n_img):
        img_of = img_of + jnp.where(place >= k * pad, 1, 0)
    rest = place - img_of * pad
    plane_of = (img_of * n_plane - 1 + rest // MOST).astype(F32)
    turn_of = (rest % MOST).astype(F32)
    take = (rest < MOST * n_pair) & (plane_of == plane_b) & (turn_of == rank_b)
    take = jnp.where(take, 1.0, 0.0).astype(BF16)

    lane_x = lax.broadcasted_iota(jnp.int32, (n_blk, LANES), 1).astype(F32)
    column_x = col_b * LANES + lane_x
    fold_x = jnp.minimum(column_x, box - column_x)
    fold_y = jnp.minimum(row_b, box - row_b)
    wave_sq = (fold_x * fold_x + fold_y * fold_y) * (1.0 / (box * box))
    ctf = -jnp.sin(CTF_SCALE * focus_b * wave_sq + CTF_PHASE) * (1.0 / box)
    source_lane = lax.broadcasted_iota(jnp.int32, (LANES, LANES), 0)
    target_lane = lax.broadcasted_iota(jnp.int32, (LANES, LANES), 1)
    low_half = source_lane < lower
    orders = []
    for offset in (
        jnp.where(low_half, 2 * source_lane, 2 * source_lane - LANES + 1),
        jnp.where(low_half, 2 * source_lane + 1, 2 * source_lane - LANES),
    ):
        orders.append(offset == target_lane)
        orders.append((offset + target_lane) % LANES == 0)
    orders = jnp.concatenate([jnp.where(v, 1.0, 0.0).astype(BF16) for v in orders], axis=1)
    mirrored_b = col_b >= float(half_blocks)
    base_b = jnp.where(mirrored_b, 2.0 * half_blocks - 1.0 - col_b, col_b)
    odd_b = base_b - 2.0 * jnp.floor(base_b * 0.5) > 0.0

    for copy in copies:
        copy.wait_recv()
    all_high, all_low = halves(recv2[...].reshape(n_sum, 2 * LANES))
    value = dot(take, all_high) + dot(take, all_low)
    for k in range(2):
        part = value[:, k * LANES : (k + 1) * LANES]
        high, low = halves(part)
        laid = dot(high, orders) + dot(low, orders)
        laid = [laid[:, v * LANES : (v + 1) * LANES] for v in range(4)]
        even = jnp.where(mirrored_b, laid[1], laid[0])
        odd = jnp.where(mirrored_b, laid[3], laid[2])
        out_ref[:, k, :] = jnp.where(odd_b, odd, even) * ctf

    for copy in copies:
        copy.wait_send()
    for g in range(n_step):
        twin_copy(g).wait_send()
        for copy in chip_copies(g):
            copy.wait_send()


def on_device(n_slab, n_img, volume, blk_plane, blk_row, blk_col, frac_plane, frac_row, defocus):
    n_plane, n_row, box = volume.shape
    n_image, img_blk = blk_plane.shape
    n_group = n_slab * n_img
    n_blk = n_image // n_group * img_blk
    n_pair = n_plane + 1
    n_slot = MOST * n_group
    tile = MOST * n_img
    per_step = max(1, min(n_plane, 256 // n_row))
    n_step = n_plane // per_step
    pad = -(-MOST * n_pair // 8) * 8
    table_high, table_low = column_table(box)
    dims = (n_slab, n_img, n_plane, n_row, box, n_group, n_blk, per_step)
    any_space = pl.BlockSpec(memory_space=pl.ANY)
    vmem = pl.BlockSpec(memory_space=pltpu.VMEM)
    out = pl.pallas_call(
        functools.partial(kernel, dims),
        out_shape=jax.ShapeDtypeStruct((n_blk, 2, LANES), F32),
        in_specs=[any_space] * 9,
        out_specs=vmem,
        scratch_shapes=[
            pltpu.VMEM((3, img_blk, n_image), jnp.int32),
            pltpu.VMEM((2, img_blk, n_image), F32),
            pltpu.VMEM((1, n_image), F32),
            pltpu.VMEM((6, n_slot, n_blk), F32),
            pltpu.VMEM((n_plane, n_row, box), F32),
            pltpu.VMEM((box // 2, box), BF16),
            pltpu.VMEM((box // 2, box), BF16),
            pltpu.VMEM(((n_plane + 2) * n_row, box), BF16),
            pltpu.VMEM(((n_plane + 2) * n_row, box), BF16),
            pltpu.VMEM((n_pair, n_slot, 2 * LANES), F32),
            pltpu.VMEM((n_pair, n_slot // CORES, 2 * LANES), F32),
            pltpu.VMEM((n_pair, n_slot // CORES, 2 * LANES), F32),
            pltpu.VMEM((n_slab // CORES - 1, n_pair, tile, 2 * LANES), F32),
            pltpu.VMEM((n_img, pad, 2 * LANES), F32),
            pltpu.VMEM((n_img, pad, 2 * LANES), F32),
            pltpu.SemaphoreType.DMA((6,)),
            pltpu.SemaphoreType.DMA((n_plane,)),
            pltpu.SemaphoreType.DMA((2,)),
            pltpu.SemaphoreType.DMA((2, n_step)),
            pltpu.SemaphoreType.DMA((n_step, n_slab // CORES - 1)),
            pltpu.SemaphoreType.DMA((n_step, n_slab // CORES - 1)),
            pltpu.SemaphoreType.DMA((n_img - 1,)),
            pltpu.SemaphoreType.DMA((n_img - 1,)),
        ],
        compiler_params=pltpu.CompilerParams(
            collective_id=0, has_side_effects=True, vmem_limit_bytes=58 * 1024 * 1024
        ),
        cost_estimate=pl.CostEstimate(flops=8_000_000_000, bytes_accessed=9_000_000, transcendentals=0),
        name="slices",
    )(
        blk_plane.T, blk_row.T, blk_col.T, frac_plane.T, frac_row.T, defocus[None, :],
        volume, jnp.asarray(table_high), jnp.asarray(table_low),
    )
    return out.reshape(n_image // n_group, img_blk, 2, LANES)


def solution(mesh):
    placed = (P("img", "slab", None), P(), P(), P(), P(), P(), P())
    return jax.shard_map(
        functools.partial(on_device, mesh.shape["slab"], mesh.shape["img"]),
        mesh=mesh,
        in_specs=placed,
        out_specs=P(("slab", "img"), None, None, None),
        check_vma=False,
    )
```

```python
import functools
import math

import jax
import jax.numpy as jnp
import ml_dtypes
import numpy as np
from jax import lax
from jax.experimental import pallas as pl
from jax.experimental.pallas import tpu as pltpu
from jax.sharding import PartitionSpec as P

LANES = 128
CTF_SCALE = 20.0
CTF_PHASE = 0.07
MOST = 2
KEY = 8192.0
CORES = 2
MESH = pl.DeviceIdType.MESH
F32 = jnp.float32
BF16 = jnp.bfloat16


def stacked(value):
    return jnp.concatenate(halves(value), axis=0)


def product(both, high, low):
    rows = both.shape[0] // 2
    wide = dot(both, high)
    return wide[:rows] + wide[rows:] + dot(both[:rows], low)


def wave_coefficients():
    grid = 0.5 * np.cos(np.linspace(0.0, np.pi, 4001))
    grid = grid[grid > 1e-6]
    basis = (4 * grid * grid)[:, None] ** np.arange(8)
    scale = 4.0 ** np.arange(8)
    cos_c = np.linalg.lstsq(basis, np.cos(2 * np.pi * grid), rcond=None)[0] * scale
    sin_c = np.linalg.lstsq(basis[:, :7] * grid[:, None], np.sin(2 * np.pi * grid), rcond=None)[0] * scale[:7]
    return [float(v) for v in cos_c], [float(v) for v in sin_c]


COS_C, SIN_C = wave_coefficients()


def horner(coefficients, value):
    total = jnp.full_like(value, coefficients[-1])
    for c in coefficients[-2::-1]:
        total = total * value + c
    return total


def wave(turns):
    part = turns - jnp.round(turns)
    square = part * part
    return horner(COS_C, square), part * horner(SIN_C, square)


def split_table(table):
    high = table.astype(ml_dtypes.bfloat16)
    low = (table - high.astype(np.float64)).astype(ml_dtypes.bfloat16)
    return high, low


def column_table(box):
    half, lower = box // 2, LANES // 2
    lane = np.arange(LANES)
    parts = []
    for u in range(half // LANES // 2):
        first = 2 * u * LANES
        even = first + 2 * lane
        odd = first + np.where(lane < lower, LANES + 2 * lane + 1, 2 * (lane - lower) + 1)
        for wanted in (even, odd):
            angle = ((np.arange(half)[:, None] * wanted[None, :]) % box) * (2.0 * np.pi / box)
            real, imag = np.cos(angle), -np.sin(angle)
            imag[:, wanted == 0] = (1.0 - 2.0 * (np.arange(half) % 2))[:, None]
            parts += [real, imag]
    return split_table(np.concatenate(parts, axis=1))


def halves(value):
    high = value.astype(BF16)
    low = (value - high.astype(F32)).astype(BF16)
    return high, low


def dot(a, b):
    return jnp.dot(a, b, preferred_element_type=F32)


def kernel(
    dims, plane_hbm, row_hbm, col_hbm, fz_hbm, fy_hbm, focus_hbm, vol_hbm, high_hbm, low_hbm, out_ref,
    ints, floats, focus_ref, meta_ref, vol, t_high, t_low, z_high, z_low, stage, recv_twin, joined, recv, red, recv2,
    meta_sem, vol_sem, tab_sem, twin_sem, send_sem, recv_sem, send2_sem, recv2_sem,
):
    n_slab, n_img, n_plane, n_row, box, n_group, n_blk, per_step = dims
    n_pair = n_plane + 1
    n_slot = MOST * n_group
    tile = MOST * n_img
    half_blocks = box // LANES // 2
    lower = LANES // 2
    n_chip = n_slab // CORES
    half_slots = n_slot // CORES
    s, i = lax.axis_index("slab"), lax.axis_index("img")
    chip, core = s // CORES, s % CORES
    twin = chip * CORES + 1 - core

    meta_copies = [
        pltpu.make_async_copy(source, target, meta_sem.at[k])
        for k, (source, target) in enumerate(
            [
                (plane_hbm, ints.at[0]), (row_hbm, ints.at[1]), (col_hbm, ints.at[2]),
                (fz_hbm, floats.at[0]), (fy_hbm, floats.at[1]), (focus_hbm, focus_ref),
            ]
        )
    ]
    tab_copies = [
        pltpu.make_async_copy(high_hbm, t_high, tab_sem.at[0]),
        pltpu.make_async_copy(low_hbm, t_low, tab_sem.at[1]),
    ]

    def vol_copy(q):
        return pltpu.make_async_copy(vol_hbm.at[q], vol.at[q], vol_sem.at[q])

    for copy in meta_copies:
        copy.start()
    tab_copies[0].start()
    for q in range(per_step):
        vol_copy(q).start()
    tab_copies[1].start()
    for q in range(per_step, n_plane):
        vol_copy(q).start()

    barrier = pltpu.get_barrier_semaphore()
    pl.semaphore_signal(barrier, inc=1, device_id=(twin, i), device_id_type=MESH)
    for d in range(1, n_chip):
        to = lax.rem(chip + d, n_chip) * CORES + core
        pl.semaphore_signal(barrier, inc=1, device_id=(to, i), device_id_type=MESH)
    for d in range(1, n_img):
        pl.semaphore_signal(barrier, inc=1, device_id=(s, lax.rem(i + d, n_img)), device_id_type=MESH)

    zero_rows = jnp.zeros((n_row, box), BF16)
    for ref in (z_high, z_low):
        ref[pl.ds(0, n_row)] = zero_rows
        ref[pl.ds((n_plane + 1) * n_row, n_row)] = zero_rows
    red[...] = jnp.zeros_like(red)

    for copy in meta_copies:
        copy.wait()
    img_blk, n_image = ints.shape[1:]
    own_images = n_image // n_group
    image = lax.broadcasted_iota(jnp.int32, (n_blk, n_image), 1)
    within = lax.broadcasted_iota(jnp.int32, (n_blk, n_image), 0) // img_blk
    in_turn = image % own_images == within
    slot_at = lax.broadcasted_iota(jnp.int32, (n_slot, n_image), 0)
    slot_core = jnp.where(slot_at >= half_slots, 1, 0)
    slot_at = slot_at - slot_core * half_slots
    slot_at = (slot_at // tile * CORES + slot_core) * n_img + slot_at % tile // MOST
    image_at = lax.broadcasted_iota(jnp.int32, (n_slot, n_image), 1) // own_images
    spread = jnp.where(slot_at == image_at, 1.0, 0.0)
    plane_of_block, row_of_block, col_of_block = [ints[k].astype(F32) for k in range(3)]
    at_image = lax.broadcasted_iota(jnp.int32, (img_blk, n_image), 1) % own_images
    seen = jnp.zeros((img_blk, n_image), F32)
    for back in range(1, own_images):
        earlier = pltpu.roll(plane_of_block, back, 1)
        for turned in range(img_blk):
            other = pltpu.roll(earlier, turned, 0) if turned else earlier
            seen = jnp.where((at_image >= back) & (other == plane_of_block), 1.0, seen)
    n_col = box // LANES
    sources = [plane_of_block + KEY * seen, row_of_block * n_col + col_of_block, floats[0], floats[1]]
    sources.append(jnp.broadcast_to(focus_ref[...], (img_blk, n_image)))
    for k, source in enumerate(sources):
        laid = jnp.where(in_turn, jnp.concatenate([source] * own_images, axis=0), 0.0)
        meta_ref[k] = lax.dot_general(
            spread, laid, (((1,), (1,)), ((), ())),
            precision=lax.Precision.HIGHEST, preferred_element_type=F32,
        )

    lane = lax.broadcasted_iota(jnp.int32, (1, n_row), 1)
    y = (lane + s * n_row).astype(F32)
    step_cos, step_sin = wave(y * (1.0 / box))
    turn = (lax.broadcasted_iota(jnp.int32, (n_slot, 1), 0) % MOST).astype(F32) * KEY

    def weights(pair):
        plane = n_plane * i - 1 + pair
        mask = meta_ref[0] == turn + plane.astype(F32)

        def pick(k):
            return jnp.sum(jnp.where(mask, meta_ref[k], 0.0), axis=1, keepdims=True)

        code, fz, fy = pick(1), pick(2), pick(3)
        row = jnp.floor(code * (1.0 / n_col))
        col = code - row * n_col
        cosine, sine = wave(row * y * (1.0 / box))
        h_real = (1.0 - fy) + fy * step_cos
        h_imag = -fy * step_sin
        g_real = cosine * h_real + sine * h_imag
        g_imag = cosine * h_imag - sine * h_real
        both = [jnp.concatenate([part * (1.0 - fz), part * fz], axis=1) for part in (g_real, g_imag)]
        return col, stacked(jnp.concatenate(both, axis=0))

    slot_lane = lax.broadcasted_iota(jnp.int32, (n_slot, LANES), 1)

    def evaluate(pair, given):
        rows = pl.ds(pair * n_row, 2 * n_row)
        if not isinstance(pair, int):
            rows = pl.ds(pl.multiple_of(pair * n_row, n_row), 2 * n_row)
        col, rows_of = given
        mirrored = col >= float(half_blocks)
        base = jnp.where(mirrored, 2.0 * half_blocks - 1.0 - col, col)
        odd = base - 2.0 * jnp.floor(base * 0.5)
        wanted = jnp.where(slot_lane < lower, base, base + 1.0 - 2.0 * odd)
        sign = jnp.where(mirrored, -1.0, 1.0)
        sign = jnp.where((slot_lane == 0) & (wanted == 0.0), 0.0, sign)
        beyond = jnp.where(base == half_blocks - 1.0, -1.0, base + odd)
        beyond = jnp.broadcast_to(beyond, (n_slot, LANES))
        real = imag = past_real = past_imag = None
        for cb in range(half_blocks):
            at = pl.ds(cb * 2 * LANES, 2 * LANES)
            prod = product(rows_of, z_high[rows, at], z_low[rows, at])
            a, b = prod[:n_slot, :LANES], prod[:n_slot, LANES:]
            c, d = prod[n_slot:, :LANES], prod[n_slot:, LANES:]
            now_real, now_imag = a - sign * d, c + sign * b
            if cb == 0:
                real, imag = now_real, now_imag
                middle = beyond == -1.0
                past_real = jnp.where(middle, b, now_real)
                past_imag = jnp.where(middle, d, now_imag)
            else:
                match = wanted == float(cb)
                real = jnp.where(match, now_real, real)
                imag = jnp.where(match, now_imag, imag)
                if cb % 2 == 0:
                    match = beyond == float(cb)
                    past_real = jnp.where(match, now_real, past_real)
                    past_imag = jnp.where(match, now_imag, past_imag)
        put = mirrored & (slot_lane == jnp.where(odd > 0.0, lower, 0))
        stage[pair, :, pl.ds(0, LANES)] = jnp.where(put, pltpu.roll(past_real, lower, 1), real)
        stage[pair, :, pl.ds(LANES, LANES)] = jnp.where(put, pltpu.roll(past_imag, lower, 1), imag)

    n_step = n_plane // per_step
    spans = [(g * per_step, per_step) for g in range(n_step)]
    spans[-1] = (spans[-1][0], per_step + 1)
    own_half = pl.multiple_of(core * half_slots, half_slots)
    other_half = pl.multiple_of((1 - core) * half_slots, half_slots)

    def twin_copy(g):
        pairs = pl.ds(*spans[g])
        return pltpu.make_async_remote_copy(
            src_ref=stage.at[pairs, pl.ds(other_half, half_slots)],
            dst_ref=recv_twin.at[pairs],
            send_sem=twin_sem.at[0, g],
            recv_sem=twin_sem.at[1, g],
            device_id=(twin, i),
            device_id_type=MESH,
        )

    def chip_copies(g):
        pairs = pl.ds(*spans[g])
        copies = []
        for d in range(1, n_chip):
            to = lax.rem(chip + d, n_chip)
            copies.append(
                pltpu.make_async_remote_copy(
                    src_ref=joined.at[pairs, pl.ds(pl.multiple_of(to * tile, tile), tile)],
                    dst_ref=recv.at[d - 1, pairs],
                    send_sem=send_sem.at[g, d - 1],
                    recv_sem=recv_sem.at[g, d - 1],
                    device_id=(to * CORES + core, i),
                    device_id_type=MESH,
                )
            )
        return copies

    def join(g):
        pairs = pl.ds(*spans[g])
        twin_copy(g).wait_recv()
        joined[pairs] = stage[pairs, pl.ds(own_half, half_slots)] + recv_twin[pairs]
        for copy in chip_copies(g):
            copy.start()

    def load(step):
        for k in range(per_step):
            vol_copy(step * per_step + k).wait()
        planes = pl.ds(step * per_step, per_step)
        near = vol[planes, :, pl.ds(0, box // 2)].reshape(per_step * n_row, box // 2)
        far = vol[planes, :, pl.ds(box // 2, box // 2)].reshape(per_step * n_row, box // 2)
        return stacked(near + far), stacked(near - far)

    def transform(step, inputs, chunks):
        rows = pl.ds((step * per_step + 1) * n_row, per_step * n_row)
        for cb in chunks:
            at = pl.ds(cb * 2 * LANES, 2 * LANES)
            z = product(inputs[cb % 2], t_high[:, at], t_low[:, at])
            zh, zl = halves(z)
            z_high[rows, at] = zh
            z_low[rows, at] = zl

    for copy in tab_copies:
        copy.wait()
    given = None
    few = per_step <= 2
    for step in range(n_step + 1):
        if step < n_step:
            inputs = load(step)
        ready = []
        if few:
            for k in range(per_step):
                if step < n_step:
                    ready.append(weights(step * per_step + k))
                    each = half_blocks // per_step
                    transform(step, inputs, range(k * each, (k + 1) * each))
                if step > 0:
                    evaluate((step - 1) * per_step + k, given[k])
            if step == n_step - 1:
                ready.append(weights(n_plane))
            if step == n_step:
                evaluate(n_plane, given[per_step])
        else:
            if step < n_step:
                transform(step, inputs, range(half_blocks))
            if step > 0:

                def body(k, carry):
                    evaluate(k, weights(k))
                    return carry

                lax.fori_loop(spans[step - 1][0], sum(spans[step - 1]), body, 0)
        given = ready
        if step == 1:
            pl.semaphore_wait(barrier, n_chip + n_img - 1)
        if step > 0:
            twin_copy(step - 1).start()
        if step > 1:
            join(step - 2)
    group = s * n_img + i
    eye = lax.broadcasted_iota(jnp.int32, (n_blk, n_blk), 0) == lax.broadcasted_iota(jnp.int32, (n_blk, n_blk), 1)
    own_line = core * half_slots + chip * tile + i * MOST
    lines = [meta_ref[k, pl.ds(own_line, 1)] for k in (0, 1, 4)]
    key_b, code_b, focus_b = [jnp.sum(jnp.where(eye, v, 0.0), axis=1, keepdims=True) for v in lines]
    row_b = jnp.floor(code_b * (1.0 / n_col))
    col_b = code_b - row_b * n_col
    pad = red.shape[1]
    n_sum = n_img * pad
    place = lax.broadcasted_iota(jnp.int32, (n_blk, n_sum), 1)
    img_of = jnp.zeros_like(place)
    for k in range(1, n_img):
        img_of = img_of + jnp.where(place >= k * pad, 1, 0)
    rest = place - img_of * pad
    key_of = (img_of * n_plane - 1 + rest // MOST).astype(F32) + (rest % MOST).astype(F32) * KEY
    take = (rest < MOST * n_pair) & (key_of == key_b)
    take = jnp.where(take, 1.0, 0.0).astype(BF16)

    lane_x = lax.broadcasted_iota(jnp.int32, (n_blk, LANES), 1).astype(F32)
    column_x = col_b * LANES + lane_x
    fold_x = jnp.minimum(column_x, box - column_x)
    fold_y = jnp.minimum(row_b, box - row_b)
    wave_sq = (fold_x * fold_x + fold_y * fold_y) * (1.0 / (box * box))
    ctf = -jnp.sin(CTF_SCALE * focus_b * wave_sq + CTF_PHASE) * (1.0 / box)
    source_lane = lax.broadcasted_iota(jnp.int32, (LANES, LANES), 0)
    target_lane = lax.broadcasted_iota(jnp.int32, (LANES, LANES), 1)
    low_half = source_lane < lower
    orders = []
    for offset in (
        jnp.where(low_half, 2 * source_lane, 2 * source_lane - LANES + 1),
        jnp.where(low_half, 2 * source_lane + 1, 2 * source_lane - LANES),
    ):
        orders.append(offset == target_lane)
        orders.append((offset + target_lane) % LANES == 0)
    orders = jnp.concatenate([jnp.where(v, 1.0, 0.0).astype(BF16) for v in orders], axis=1)
    mirrored_b = col_b >= float(half_blocks)
    base_b = jnp.where(mirrored_b, 2.0 * half_blocks - 1.0 - col_b, col_b)
    odd_b = base_b - 2.0 * jnp.floor(base_b * 0.5) > 0.0

    join(n_step - 1)

    own = pl.ds(pl.multiple_of(chip * tile, tile), tile)
    for g in range(n_step):
        for copy in chip_copies(g):
            copy.wait_recv()
        for pair in range(spans[g][0], sum(spans[g])):
            total = joined[pair, own]
            for d in range(n_chip - 1):
                total = total + recv[d, pair]
            for to in range(n_img):
                red[to, pl.ds(MOST * pair, MOST)] = total[MOST * to : MOST * to + MOST]

    copies = []
    for d in range(1, n_img):
        to = lax.rem(i + d, n_img)
        copies.append(
            pltpu.make_async_remote_copy(
                src_ref=red.at[to],
                dst_ref=recv2.at[i],
                send_sem=send2_sem.at[d - 1],
                recv_sem=recv2_sem.at[d - 1],
                device_id=(s, to),
                device_id_type=MESH,
            )
        )
    for copy in copies:
        copy.start()
    recv2[i] = red[i]

    for copy in copies:
        copy.wait_recv()
    all_high, all_low = halves(recv2[...].reshape(n_sum, 2 * LANES))
    value = dot(take, all_high) + dot(take, all_low)
    for k in range(2):
        part = value[:, k * LANES : (k + 1) * LANES]
        high, low = halves(part)
        laid = dot(high, orders) + dot(low, orders)
        laid = [laid[:, v * LANES : (v + 1) * LANES] for v in range(4)]
        even = jnp.where(mirrored_b, laid[1], laid[0])
        odd = jnp.where(mirrored_b, laid[3], laid[2])
        out_ref[:, k, :] = jnp.where(odd_b, odd, even) * ctf

    for copy in copies:
        copy.wait_send()
    for g in range(n_step):
        twin_copy(g).wait_send()
        for copy in chip_copies(g):
            copy.wait_send()


def on_device(n_slab, n_img, volume, blk_plane, blk_row, blk_col, frac_plane, frac_row, defocus):
    n_plane, n_row, box = volume.shape
    n_image, img_blk = blk_plane.shape
    n_group = n_slab * n_img
    n_blk = n_image // n_group * img_blk
    n_pair = n_plane + 1
    n_slot = MOST * n_group
    tile = MOST * n_img
    per_step = max(1, min(n_plane, 256 // n_row))
    n_step = n_plane // per_step
    pad = -(-MOST * n_pair // 8) * 8
    table_high, table_low = column_table(box)
    dims = (n_slab, n_img, n_plane, n_row, box, n_group, n_blk, per_step)
    any_space = pl.BlockSpec(memory_space=pl.ANY)
    vmem = pl.BlockSpec(memory_space=pltpu.VMEM)
    out = pl.pallas_call(
        functools.partial(kernel, dims),
        out_shape=jax.ShapeDtypeStruct((n_blk, 2, LANES), F32),
        in_specs=[any_space] * 9,
        out_specs=vmem,
        scratch_shapes=[
            pltpu.VMEM((3, img_blk, n_image), jnp.int32),
            pltpu.VMEM((2, img_blk, n_image), F32),
            pltpu.VMEM((1, n_image), F32),
            pltpu.VMEM((5, n_slot, n_blk), F32),
            pltpu.VMEM((n_plane, n_row, box), F32),
            pltpu.VMEM((box // 2, box), BF16),
            pltpu.VMEM((box // 2, box), BF16),
            pltpu.VMEM(((n_plane + 2) * n_row, box), BF16),
            pltpu.VMEM(((n_plane + 2) * n_row, box), BF16),
            pltpu.VMEM((n_pair, n_slot, 2 * LANES), F32),
            pltpu.VMEM((n_pair, n_slot // CORES, 2 * LANES), F32),
            pltpu.VMEM((n_pair, n_slot // CORES, 2 * LANES), F32),
            pltpu.VMEM((n_slab // CORES - 1, n_pair, tile, 2 * LANES), F32),
            pltpu.VMEM((n_img, pad, 2 * LANES), F32),
            pltpu.VMEM((n_img, pad, 2 * LANES), F32),
            pltpu.SemaphoreType.DMA((6,)),
            pltpu.SemaphoreType.DMA((n_plane,)),
            pltpu.SemaphoreType.DMA((2,)),
            pltpu.SemaphoreType.DMA((2, n_step)),
            pltpu.SemaphoreType.DMA((n_step, n_slab // CORES - 1)),
            pltpu.SemaphoreType.DMA((n_step, n_slab // CORES - 1)),
            pltpu.SemaphoreType.DMA((n_img - 1,)),
            pltpu.SemaphoreType.DMA((n_img - 1,)),
        ],
        compiler_params=pltpu.CompilerParams(
            collective_id=0, has_side_effects=True, vmem_limit_bytes=58 * 1024 * 1024
        ),
        cost_estimate=pl.CostEstimate(flops=8_000_000_000, bytes_accessed=9_000_000, transcendentals=0),
        name="slices",
    )(
        blk_plane.T, blk_row.T, blk_col.T, frac_plane.T, frac_row.T, defocus[None, :],
        volume, jnp.asarray(table_high), jnp.asarray(table_low),
    )
    return out.reshape(n_image // n_group, img_blk, 2, LANES)


def solution(mesh):
    placed = (P("img", "slab", None), P(), P(), P(), P(), P(), P())
    return jax.shard_map(
        functools.partial(on_device, mesh.shape["slab"], mesh.shape["img"]),
        mesh=mesh,
        in_specs=placed,
        out_specs=P(("slab", "img"), None, None, None),
        check_vma=False,
    )
```

```python
import functools
import math

import jax
import jax.numpy as jnp
import ml_dtypes
import numpy as np
from jax import lax
from jax.experimental import pallas as pl
from jax.experimental.pallas import tpu as pltpu
from jax.sharding import PartitionSpec as P

LANES = 128
CTF_SCALE = 20.0
CTF_PHASE = 0.07
MOST = 2
KEY = 8192.0
CORES = 2
MESH = pl.DeviceIdType.MESH
F32 = jnp.float32
BF16 = jnp.bfloat16


def stacked(value):
    return jnp.concatenate(halves(value), axis=0)


def product(both, high, low):
    rows = both.shape[0] // 2
    wide = dot(both, high)
    return wide[:rows] + wide[rows:] + dot(both[:rows], low)


def wave_coefficients():
    grid = 0.5 * np.cos(np.linspace(0.0, np.pi, 4001))
    grid = grid[grid > 1e-6]
    basis = (4 * grid * grid)[:, None] ** np.arange(8)
    scale = 4.0 ** np.arange(8)
    cos_c = np.linalg.lstsq(basis, np.cos(2 * np.pi * grid), rcond=None)[0] * scale
    sin_c = np.linalg.lstsq(basis[:, :7] * grid[:, None], np.sin(2 * np.pi * grid), rcond=None)[0] * scale[:7]
    return [float(v) for v in cos_c], [float(v) for v in sin_c]


COS_C, SIN_C = wave_coefficients()


def horner(coefficients, value):
    total = jnp.full_like(value, coefficients[-1])
    for c in coefficients[-2::-1]:
        total = total * value + c
    return total


def wave(turns):
    part = turns - jnp.round(turns)
    square = part * part
    return horner(COS_C, square), part * horner(SIN_C, square)


def split_table(table):
    high = table.astype(ml_dtypes.bfloat16)
    low = (table - high.astype(np.float64)).astype(ml_dtypes.bfloat16)
    return high, low


def column_table(box):
    half, lower = box // 2, LANES // 2
    lane = np.arange(LANES)
    parts = []
    for u in range(half // LANES // 2):
        first = 2 * u * LANES
        even = first + 2 * lane
        odd = first + np.where(lane < lower, LANES + 2 * lane + 1, 2 * (lane - lower) + 1)
        for wanted in (even, odd):
            angle = ((np.arange(half)[:, None] * wanted[None, :]) % box) * (2.0 * np.pi / box)
            real, imag = np.cos(angle), -np.sin(angle)
            imag[:, wanted == 0] = (1.0 - 2.0 * (np.arange(half) % 2))[:, None]
            parts += [real, imag]
    return split_table(np.concatenate(parts, axis=1))


def halves(value):
    high = value.astype(BF16)
    low = (value - high.astype(F32)).astype(BF16)
    return high, low


def dot(a, b):
    return jnp.dot(a, b, preferred_element_type=F32)


def kernel(
    dims, plane_hbm, row_hbm, col_hbm, fz_hbm, fy_hbm, focus_hbm, vol_hbm, high_hbm, low_hbm, out_ref,
    ints, floats, focus_ref, meta_ref, vol, t_high, t_low, z_high, z_low, stage, recv_twin, joined, recv, red, recv2,
    meta_sem, vol_sem, tab_sem, twin_sem, send_sem, recv_sem, send2_sem, recv2_sem,
):
    n_slab, n_img, n_plane, n_row, box, n_group, n_blk, per_step = dims
    n_pair = n_plane + 1
    n_slot = MOST * n_group
    tile = MOST * n_img
    half_blocks = box // LANES // 2
    lower = LANES // 2
    n_chip = n_slab // CORES
    half_slots = n_slot // CORES
    s, i = lax.axis_index("slab"), lax.axis_index("img")
    chip, core = s // CORES, s % CORES
    twin = chip * CORES + 1 - core

    meta_copies = [
        pltpu.make_async_copy(source, target, meta_sem.at[k])
        for k, (source, target) in enumerate(
            [
                (plane_hbm, ints.at[0]), (row_hbm, ints.at[1]), (col_hbm, ints.at[2]),
                (fz_hbm, floats.at[0]), (fy_hbm, floats.at[1]), (focus_hbm, focus_ref),
            ]
        )
    ]
    tab_copies = [
        pltpu.make_async_copy(high_hbm, t_high, tab_sem.at[0]),
        pltpu.make_async_copy(low_hbm, t_low, tab_sem.at[1]),
    ]

    def vol_copy(q):
        return pltpu.make_async_copy(vol_hbm.at[q], vol.at[q], vol_sem.at[q])

    for copy in meta_copies:
        copy.start()
    tab_copies[0].start()
    for q in range(per_step):
        vol_copy(q).start()
    tab_copies[1].start()

    barrier = pltpu.get_barrier_semaphore()
    pl.semaphore_signal(barrier, inc=1, device_id=(twin, i), device_id_type=MESH)
    for d in range(1, n_chip):
        to = lax.rem(chip + d, n_chip) * CORES + core
        pl.semaphore_signal(barrier, inc=1, device_id=(to, i), device_id_type=MESH)
    for d in range(1, n_img):
        pl.semaphore_signal(barrier, inc=1, device_id=(s, lax.rem(i + d, n_img)), device_id_type=MESH)

    zero_rows = jnp.zeros((n_row, box), BF16)
    for ref in (z_high, z_low):
        ref[pl.ds(0, n_row)] = zero_rows
        ref[pl.ds((n_plane + 1) * n_row, n_row)] = zero_rows
    red[...] = jnp.zeros_like(red)

    for copy in meta_copies:
        copy.wait()
    img_blk, n_image = ints.shape[1:]
    own_images = n_image // n_group
    image = lax.broadcasted_iota(jnp.int32, (n_blk, n_image), 1)
    within = lax.broadcasted_iota(jnp.int32, (n_blk, n_image), 0) // img_blk
    in_turn = image % own_images == within
    slot_at = lax.broadcasted_iota(jnp.int32, (n_slot, n_image), 0)
    slot_core = jnp.where(slot_at >= half_slots, 1, 0)
    slot_at = slot_at - slot_core * half_slots
    slot_at = (slot_at // tile * CORES + slot_core) * n_img + slot_at % tile // MOST
    image_at = lax.broadcasted_iota(jnp.int32, (n_slot, n_image), 1) // own_images
    spread = jnp.where(slot_at == image_at, 1.0, 0.0)
    plane_of_block, row_of_block, col_of_block = [ints[k].astype(F32) for k in range(3)]
    at_image = lax.broadcasted_iota(jnp.int32, (img_blk, n_image), 1) % own_images
    seen = jnp.zeros((img_blk, n_image), F32)
    for back in range(1, own_images):
        earlier = pltpu.roll(plane_of_block, back, 1)
        for turned in range(img_blk):
            other = pltpu.roll(earlier, turned, 0) if turned else earlier
            seen = jnp.where((at_image >= back) & (other == plane_of_block), 1.0, seen)
    n_col = box // LANES
    sources = [plane_of_block + KEY * seen, row_of_block * n_col + col_of_block, floats[0], floats[1]]
    sources.append(jnp.broadcast_to(focus_ref[...], (img_blk, n_image)))
    for k, source in enumerate(sources):
        laid = jnp.where(in_turn, jnp.concatenate([source] * own_images, axis=0), 0.0)
        meta_ref[k] = lax.dot_general(
            spread, laid, (((1,), (1,)), ((), ())),
            precision=lax.Precision.HIGHEST, preferred_element_type=F32,
        )

    lane = lax.broadcasted_iota(jnp.int32, (1, n_row), 1)
    y = (lane + s * n_row).astype(F32)
    step_cos, step_sin = wave(y * (1.0 / box))
    turn = (lax.broadcasted_iota(jnp.int32, (n_slot, 1), 0) % MOST).astype(F32) * KEY

    def weights(pair):
        plane = n_plane * i - 1 + pair
        mask = meta_ref[0] == turn + plane.astype(F32)

        def pick(k):
            return jnp.sum(jnp.where(mask, meta_ref[k], 0.0), axis=1, keepdims=True)

        code, fz, fy = pick(1), pick(2), pick(3)
        row = jnp.floor(code * (1.0 / n_col))
        col = code - row * n_col
        cosine, sine = wave(row * y * (1.0 / box))
        h_real = (1.0 - fy) + fy * step_cos
        h_imag = -fy * step_sin
        g_real = cosine * h_real + sine * h_imag
        g_imag = cosine * h_imag - sine * h_real
        both = [jnp.concatenate([part * (1.0 - fz), part * fz], axis=1) for part in (g_real, g_imag)]
        return col, stacked(jnp.concatenate(both, axis=0))

    slot_lane = lax.broadcasted_iota(jnp.int32, (n_slot, LANES), 1)

    def evaluate(pair, given):
        rows = pl.ds(pair * n_row, 2 * n_row)
        if not isinstance(pair, int):
            rows = pl.ds(pl.multiple_of(pair * n_row, n_row), 2 * n_row)
        col, rows_of = given
        mirrored = col >= float(half_blocks)
        base = jnp.where(mirrored, 2.0 * half_blocks - 1.0 - col, col)
        odd = base - 2.0 * jnp.floor(base * 0.5)
        wanted = jnp.where(slot_lane < lower, base, base + 1.0 - 2.0 * odd)
        sign = jnp.where(mirrored, -1.0, 1.0)
        sign = jnp.where((slot_lane == 0) & (wanted == 0.0), 0.0, sign)
        beyond = jnp.where(base == half_blocks - 1.0, -1.0, base + odd)
        beyond = jnp.broadcast_to(beyond, (n_slot, LANES))
        real = imag = past_real = past_imag = None
        for cb in range(half_blocks):
            at = pl.ds(cb * 2 * LANES, 2 * LANES)
            prod = product(rows_of, z_high[rows, at], z_low[rows, at])
            a, b = prod[:n_slot, :LANES], prod[:n_slot, LANES:]
            c, d = prod[n_slot:, :LANES], prod[n_slot:, LANES:]
            now_real, now_imag = a - sign * d, c + sign * b
            if cb == 0:
                real, imag = now_real, now_imag
                middle = beyond == -1.0
                past_real = jnp.where(middle, b, now_real)
                past_imag = jnp.where(middle, d, now_imag)
            else:
                match = wanted == float(cb)
                real = jnp.where(match, now_real, real)
                imag = jnp.where(match, now_imag, imag)
                if cb % 2 == 0:
                    match = beyond == float(cb)
                    past_real = jnp.where(match, now_real, past_real)
                    past_imag = jnp.where(match, now_imag, past_imag)
        put = mirrored & (slot_lane == jnp.where(odd > 0.0, lower, 0))
        stage[pair, :, pl.ds(0, LANES)] = jnp.where(put, pltpu.roll(past_real, lower, 1), real)
        stage[pair, :, pl.ds(LANES, LANES)] = jnp.where(put, pltpu.roll(past_imag, lower, 1), imag)

    n_step = n_plane // per_step
    spans = [(g * per_step, per_step) for g in range(n_step)]
    spans[-1] = (spans[-1][0], per_step + 1)
    own_half = pl.multiple_of(core * half_slots, half_slots)
    other_half = pl.multiple_of((1 - core) * half_slots, half_slots)

    def twin_copy(g):
        pairs = pl.ds(*spans[g])
        return pltpu.make_async_remote_copy(
            src_ref=stage.at[pairs, pl.ds(other_half, half_slots)],
            dst_ref=recv_twin.at[pairs],
            send_sem=twin_sem.at[0, g],
            recv_sem=twin_sem.at[1, g],
            device_id=(twin, i),
            device_id_type=MESH,
        )

    def chip_copies(g):
        pairs = pl.ds(*spans[g])
        copies = []
        for d in range(1, n_chip):
            to = lax.rem(chip + d, n_chip)
            copies.append(
                pltpu.make_async_remote_copy(
                    src_ref=joined.at[pairs, pl.ds(pl.multiple_of(to * tile, tile), tile)],
                    dst_ref=recv.at[d - 1, pairs],
                    send_sem=send_sem.at[g, d - 1],
                    recv_sem=recv_sem.at[g, d - 1],
                    device_id=(to * CORES + core, i),
                    device_id_type=MESH,
                )
            )
        return copies

    def join(g):
        pairs = pl.ds(*spans[g])
        twin_copy(g).wait_recv()
        joined[pairs] = stage[pairs, pl.ds(own_half, half_slots)] + recv_twin[pairs]
        for copy in chip_copies(g):
            copy.start()

    def load(step):
        for k in range(per_step):
            vol_copy(step * per_step + k).wait()
        planes = pl.ds(step * per_step, per_step)
        near = vol[planes, :, pl.ds(0, box // 2)].reshape(per_step * n_row, box // 2)
        far = vol[planes, :, pl.ds(box // 2, box // 2)].reshape(per_step * n_row, box // 2)
        return stacked(near + far), stacked(near - far)

    def transform(step, inputs, chunks):
        rows = pl.ds((step * per_step + 1) * n_row, per_step * n_row)
        for cb in chunks:
            at = pl.ds(cb * 2 * LANES, 2 * LANES)
            z = product(inputs[cb % 2], t_high[:, at], t_low[:, at])
            zh, zl = halves(z)
            z_high[rows, at] = zh
            z_low[rows, at] = zl

    for copy in tab_copies:
        copy.wait()
    for q in range(per_step, n_plane):
        vol_copy(q).start()
    given = None
    few = per_step <= 2
    for step in range(n_step + 1):
        if step < n_step:
            inputs = load(step)
        ready = []
        if few:
            for k in range(per_step):
                if step < n_step:
                    ready.append(weights(step * per_step + k))
                    each = half_blocks // per_step
                    transform(step, inputs, range(k * each, (k + 1) * each))
                if step > 0:
                    evaluate((step - 1) * per_step + k, given[k])
            if step == n_step - 1:
                ready.append(weights(n_plane))
            if step == n_step:
                evaluate(n_plane, given[per_step])
        else:
            if step < n_step:
                transform(step, inputs, range(half_blocks))
            if step > 0:

                def body(k, carry):
                    evaluate(k, weights(k))
                    return carry

                lax.fori_loop(spans[step - 1][0], sum(spans[step - 1]), body, 0)
        given = ready
        if step == 1:
            pl.semaphore_wait(barrier, n_chip + n_img - 1)
        if step > 0:
            twin_copy(step - 1).start()
        if step > 1:
            join(step - 2)
    group = s * n_img + i
    eye = lax.broadcasted_iota(jnp.int32, (n_blk, n_blk), 0) == lax.broadcasted_iota(jnp.int32, (n_blk, n_blk), 1)
    own_line = core * half_slots + chip * tile + i * MOST
    lines = [meta_ref[k, pl.ds(own_line, 1)] for k in (0, 1, 4)]
    key_b, code_b, focus_b = [jnp.sum(jnp.where(eye, v, 0.0), axis=1, keepdims=True) for v in lines]
    row_b = jnp.floor(code_b * (1.0 / n_col))
    col_b = code_b - row_b * n_col
    pad = red.shape[1]
    n_sum = n_img * pad
    place = lax.broadcasted_iota(jnp.int32, (n_blk, n_sum), 1)
    img_of = jnp.zeros_like(place)
    for k in range(1, n_img):
        img_of = img_of + jnp.where(place >= k * pad, 1, 0)
    rest = place - img_of * pad
    key_of = (img_of * n_plane - 1 + rest // MOST).astype(F32) + (rest % MOST).astype(F32) * KEY
    take = (rest < MOST * n_pair) & (key_of == key_b)
    take = jnp.where(take, 1.0, 0.0).astype(BF16)

    lane_x = lax.broadcasted_iota(jnp.int32, (n_blk, LANES), 1).astype(F32)
    column_x = col_b * LANES + lane_x
    fold_x = jnp.minimum(column_x, box - column_x)
    fold_y = jnp.minimum(row_b, box - row_b)
    wave_sq = (fold_x * fold_x + fold_y * fold_y) * (1.0 / (box * box))
    ctf = -jnp.sin(CTF_SCALE * focus_b * wave_sq + CTF_PHASE) * (1.0 / box)
    source_lane = lax.broadcasted_iota(jnp.int32, (LANES, LANES), 0)
    target_lane = lax.broadcasted_iota(jnp.int32, (LANES, LANES), 1)
    low_half = source_lane < lower
    orders = []
    for offset in (
        jnp.where(low_half, 2 * source_lane, 2 * source_lane - LANES + 1),
        jnp.where(low_half, 2 * source_lane + 1, 2 * source_lane - LANES),
    ):
        orders.append(offset == target_lane)
        orders.append((offset + target_lane) % LANES == 0)
    orders = jnp.concatenate([jnp.where(v, 1.0, 0.0).astype(BF16) for v in orders], axis=1)
    mirrored_b = col_b >= float(half_blocks)
    base_b = jnp.where(mirrored_b, 2.0 * half_blocks - 1.0 - col_b, col_b)
    odd_b = base_b - 2.0 * jnp.floor(base_b * 0.5) > 0.0

    join(n_step - 1)

    own = pl.ds(pl.multiple_of(chip * tile, tile), tile)
    for g in range(n_step):
        for copy in chip_copies(g):
            copy.wait_recv()
        for pair in range(spans[g][0], sum(spans[g])):
            total = joined[pair, own]
            for d in range(n_chip - 1):
                total = total + recv[d, pair]
            for to in range(n_img):
                red[to, pl.ds(MOST * pair, MOST)] = total[MOST * to : MOST * to + MOST]

    copies = []
    for d in range(1, n_img):
        to = lax.rem(i + d, n_img)
        copies.append(
            pltpu.make_async_remote_copy(
                src_ref=red.at[to],
                dst_ref=recv2.at[i],
                send_sem=send2_sem.at[d - 1],
                recv_sem=recv2_sem.at[d - 1],
                device_id=(s, to),
                device_id_type=MESH,
            )
        )
    for copy in copies:
        copy.start()
    recv2[i] = red[i]

    for copy in copies:
        copy.wait_recv()
    all_high, all_low = halves(recv2[...].reshape(n_sum, 2 * LANES))
    value = dot(take, all_high) + dot(take, all_low)
    for k in range(2):
        part = value[:, k * LANES : (k + 1) * LANES]
        high, low = halves(part)
        laid = dot(high, orders) + dot(low, orders)
        laid = [laid[:, v * LANES : (v + 1) * LANES] for v in range(4)]
        even = jnp.where(mirrored_b, laid[1], laid[0])
        odd = jnp.where(mirrored_b, laid[3], laid[2])
        out_ref[:, k, :] = jnp.where(odd_b, odd, even) * ctf

    for copy in copies:
        copy.wait_send()
    for g in range(n_step):
        twin_copy(g).wait_send()
        for copy in chip_copies(g):
            copy.wait_send()


def on_device(n_slab, n_img, volume, blk_plane, blk_row, blk_col, frac_plane, frac_row, defocus):
    n_plane, n_row, box = volume.shape
    n_image, img_blk = blk_plane.shape
    n_group = n_slab * n_img
    n_blk = n_image // n_group * img_blk
    n_pair = n_plane + 1
    n_slot = MOST * n_group
    tile = MOST * n_img
    per_step = max(1, min(n_plane, 256 // n_row))
    n_step = n_plane // per_step
    pad = -(-MOST * n_pair // 8) * 8
    table_high, table_low = column_table(box)
    dims = (n_slab, n_img, n_plane, n_row, box, n_group, n_blk, per_step)
    any_space = pl.BlockSpec(memory_space=pl.ANY)
    vmem = pl.BlockSpec(memory_space=pltpu.VMEM)
    out = pl.pallas_call(
        functools.partial(kernel, dims),
        out_shape=jax.ShapeDtypeStruct((n_blk, 2, LANES), F32),
        in_specs=[any_space] * 9,
        out_specs=vmem,
        scratch_shapes=[
            pltpu.VMEM((3, img_blk, n_image), jnp.int32),
            pltpu.VMEM((2, img_blk, n_image), F32),
            pltpu.VMEM((1, n_image), F32),
            pltpu.VMEM((5, n_slot, n_blk), F32),
            pltpu.VMEM((n_plane, n_row, box), F32),
            pltpu.VMEM((box // 2, box), BF16),
            pltpu.VMEM((box // 2, box), BF16),
            pltpu.VMEM(((n_plane + 2) * n_row, box), BF16),
            pltpu.VMEM(((n_plane + 2) * n_row, box), BF16),
            pltpu.VMEM((n_pair, n_slot, 2 * LANES), F32),
            pltpu.VMEM((n_pair, n_slot // CORES, 2 * LANES), F32),
            pltpu.VMEM((n_pair, n_slot // CORES, 2 * LANES), F32),
            pltpu.VMEM((n_slab // CORES - 1, n_pair, tile, 2 * LANES), F32),
            pltpu.VMEM((n_img, pad, 2 * LANES), F32),
            pltpu.VMEM((n_img, pad, 2 * LANES), F32),
            pltpu.SemaphoreType.DMA((6,)),
            pltpu.SemaphoreType.DMA((n_plane,)),
            pltpu.SemaphoreType.DMA((2,)),
            pltpu.SemaphoreType.DMA((2, n_step)),
            pltpu.SemaphoreType.DMA((n_step, n_slab // CORES - 1)),
            pltpu.SemaphoreType.DMA((n_step, n_slab // CORES - 1)),
            pltpu.SemaphoreType.DMA((n_img - 1,)),
            pltpu.SemaphoreType.DMA((n_img - 1,)),
        ],
        compiler_params=pltpu.CompilerParams(
            collective_id=0, has_side_effects=True, vmem_limit_bytes=58 * 1024 * 1024
        ),
        cost_estimate=pl.CostEstimate(flops=8_000_000_000, bytes_accessed=9_000_000, transcendentals=0),
        name="slices",
    )(
        blk_plane.T, blk_row.T, blk_col.T, frac_plane.T, frac_row.T, defocus[None, :],
        volume, jnp.asarray(table_high), jnp.asarray(table_low),
    )
    return out.reshape(n_image // n_group, img_blk, 2, LANES)


def solution(mesh):
    placed = (P("img", "slab", None), P(), P(), P(), P(), P(), P())
    return jax.shard_map(
        functools.partial(on_device, mesh.shape["slab"], mesh.shape["img"]),
        mesh=mesh,
        in_specs=placed,
        out_specs=P(("slab", "img"), None, None, None),
        check_vma=False,
    )
```
